128 devices in a mesh: seq: 16 (over z, x), head: 8 (over y, core).
Axes of the slice: x: 4, y: 4, z: 4, core: 2. Of those that a mesh axis runs over, the one named last changes fastest.
Arguments:
- hidden: bfloat16 [8192, 8192], P('seq', 'head'), may hold values from -6 to 6
- w_query: bfloat16 [8192, 4096], P(None, 'head'), may hold values from -0.0625 to 0.0625
- w_key: bfloat16 [8192, 1024], P(None, 'head'), may hold values from -0.0625 to 0.0625
- w_value: bfloat16 [8192, 1024], P(None, 'head'), may hold values from -0.0625 to 0.0625
- w_out: bfloat16 [4096, 8192], P('head'), may hold values from -0.125 to 0.125
- prefix_keys: bfloat16 [65536, 1024], P('seq', 'head'), may hold values from -300 to 300
- prefix_values: bfloat16 [65536, 1024], P('seq', 'head'), may hold values from -6 to 6
- seg_lengths: int32 [256], replicated, may hold values from 1 to 256, as said below
- ancestors: int32 [64, 4], replicated, may hold values from -1 to 255, as said below
Outputs:
- attn_out: bfloat16 [8192, 8192], P('seq', 'head')
The draws below stay inside these ranges and needn't reach their ends.
Inputs may be any that keep to these rules, and one draw needn't show every extreme that they name: `seg_lengths`: entry 0 is 256. `ancestors`: entry l of a row is -1 or a segment whose index is l modulo 4; entry 0 is never -1; the non-negative entries come first, and each descends from the one before.
All inputs are finite; a program needn't handle non-finite values.
Results may differ from the reference program's by a relative error of at most 0.02.
Values may be sent and summed in bfloat16 or wider, within the bound.
No kernel may reach another device: no remote copies, remote signals or barrier semaphores. Data moves between devices by JAX's collectives and lax.ppermute only.
A program may use at most 192 MiB of HBM per device.

```python
import math
import jax
import jax.numpy as jnp
from jax import lax

D = 8192
QH = 32
KVH = 8
HD = 128
ROLL = 128
SEG_LEN = 256
DEPTH = 4
LEAVES = 8192
ROLLS = 64
NSEG = 256
PREFIX = 65536


def draw_prefix_keys(key, part):
    key = jax.random.fold_in(key, 11)
    key_base = jax.random.fold_in(key, 0)
    base = jax.random.normal(key_base, (PREFIX, KVH * HD), jnp.float32)
    return jnp.clip(base, -300.0, 300.0).astype(jnp.bfloat16)


def draw_seg_lengths(key, part):
    key = jax.random.fold_in(key, 12)
    lengths = jax.random.randint(key, (NSEG,), 1, SEG_LEN + 1, dtype=jnp.int32)
    return lengths.at[0].set(SEG_LEN)


def draw_ancestors(key, part):
    key = jax.random.fold_in(key, 13)
    key_parent, key_leaf, key_depth = jax.random.split(key, 3)
    per_level = NSEG // DEPTH
    parent_slot = jax.random.randint(key_parent, (NSEG,), 0, per_level, dtype=jnp.int32)
    current = DEPTH - 1 + DEPTH * jax.random.randint(key_leaf, (ROLLS,), 0, per_level, dtype=jnp.int32)
    columns = [current]
    for level in range(DEPTH - 2, -1, -1):
        current = level + DEPTH * parent_slot[current]
        columns.insert(0, current)
    path = jnp.stack(columns, axis=1)
    depths = jax.random.randint(key_depth, (ROLLS, 1), 1, DEPTH + 1, dtype=jnp.int32)
    levels = jnp.arange(DEPTH, dtype=jnp.int32)[None, :]
    return jnp.where(levels < depths, path, -1).astype(jnp.int32)


def with_spikes(array, own_key, source, target, blocks, factor):
    owner, partner = [(jnp.arange(array.shape[position]) // (array.shape[position] // blocks)).reshape([-1 if axis == position else 1 for axis in range(array.ndim)]) for position in (source, target)]
    chosen = jax.random.permutation(own_key, blocks)[partner]
    strong = (owner == chosen) | (owner == (partner + blocks // 2) % blocks)
    return jnp.where(strong, factor * array, array)


def steps_of(rng, shape, shards, least, top_value):
    level = 1.0
    for dim, shards_of in shards:
        heights = jax.random.uniform(jax.random.fold_in(jax.random.fold_in(rng, 6), dim), (shards_of,), jnp.float32, least / len(shards), top_value / len(shards))
        level = level * jnp.repeat(jnp.exp(heights), shape[dim] // shards_of).reshape((-1,) + (1,) * (len(shape) - 1 - dim))
    return level


def gaussian(stream_key, shape, spread, reach, shards=(), kind=jnp.bfloat16):
    entries = jax.random.normal(stream_key, shape, jnp.float32) * spread
    if len(shards) > 0:
        entries = steps_of(stream_key, shape, shards, -0.22, 0.18) * entries
    return jnp.clip(entries, min=-reach, max=reach).astype(kind)


def noise_with(stream_key, dims, deviation, limit, pieces, heavy, kind=jnp.bfloat16):
    entries = deviation * jax.random.normal(stream_key, dims, jnp.float32)
    if pieces:
        entries = entries * steps_of(stream_key, dims, pieces, -0.22, 0.18)
    return jnp.clip(with_spikes(entries, jax.random.fold_in(stream_key, 3), *heavy), -limit, limit).astype(kind)


def setup_inputs(seed: int = 0) -> dict:
    streams_of = jax.random.split(jax.random.key(seed), 10)
    hidden = gaussian(streams_of[0], (LEAVES, D), 1.0, 6.0, ((0, 16), (1, 8)))
    w_query = gaussian(streams_of[1], (D, QH * HD), D ** -0.5, 0.0625, ((1, 8),))
    w_key = gaussian(streams_of[2], (D, KVH * HD), D ** -0.5, 0.0625, ((1, 8),))
    w_value = gaussian(streams_of[3], (D, KVH * HD), D ** -0.5, 0.0625, ((1, 8),))
    w_out = noise_with(streams_of[4], (QH * HD, D), (QH * HD) ** -0.5, 0.125, ((0, 8),), (0, 1, 8, 2.0))
    prefix_keys = draw_prefix_keys(jax.random.fold_in(streams_of[9], 71), 0)
    prefix_values = gaussian(streams_of[6], (PREFIX, KVH * HD), 1.0, 6.0, ((0, 16), (1, 8)))
    seg_lengths = draw_seg_lengths(jax.random.fold_in(streams_of[9], 71), 0)
    ancestors = draw_ancestors(jax.random.fold_in(streams_of[9], 71), 0)
    return {"hidden": hidden, "w_query": w_query, "w_key": w_key, "w_value": w_value, "w_out": w_out, "prefix_keys": prefix_keys, "prefix_values": prefix_values, "seg_lengths": seg_lengths, "ancestors": ancestors}


def reference(hidden, w_query, w_key, w_value, w_out, prefix_keys, prefix_values, seg_lengths, ancestors):
    per_group = QH // KVH
    inv_root = 1.0 / math.sqrt(HD)
    queries = jnp.dot(hidden, w_query, preferred_element_type=jnp.float32).astype(jnp.bfloat16)
    leaf_keys = jnp.dot(hidden, w_key, preferred_element_type=jnp.float32).astype(jnp.bfloat16)
    leaf_values = jnp.dot(hidden, w_value, preferred_element_type=jnp.float32).astype(jnp.bfloat16)
    query_rolls = queries.reshape(ROLLS, ROLL, KVH, per_group, HD)
    key_rolls = leaf_keys.reshape(ROLLS, ROLL, KVH, HD)
    value_rolls = leaf_values.reshape(ROLLS, ROLL, KVH, HD)
    seg_keys = prefix_keys.reshape(NSEG, SEG_LEN, KVH, HD)
    seg_values = prefix_values.reshape(NSEG, SEG_LEN, KVH, HD)
    slot_ids = jnp.arange(SEG_LEN, dtype=jnp.int32)
    causal = jnp.arange(ROLL)[:, None] >= jnp.arange(ROLL)[None, :]

    def attend_rollout(items):
        query_block, key_block, value_block, chain = items
        picked = jnp.maximum(chain, 0).astype(jnp.int32)
        far_keys = seg_keys[picked].reshape(DEPTH * SEG_LEN, KVH, HD)
        far_values = seg_values[picked].reshape(DEPTH * SEG_LEN, KVH, HD)
        live_slots = (chain[:, None] >= 0) & (slot_ids[None, :] < seg_lengths[picked][:, None])
        live_slots = jnp.broadcast_to(live_slots.reshape(1, DEPTH * SEG_LEN), (ROLL, DEPTH * SEG_LEN))
        allowed = jnp.concatenate([live_slots, causal], axis=1)
        all_keys = jnp.concatenate([far_keys, key_block], axis=0)
        all_values = jnp.concatenate([far_values, value_block], axis=0)
        scores = jnp.einsum('rkgd,nkd->kgrn', query_block.astype(jnp.float32), all_keys.astype(jnp.float32)) * inv_root
        scores = jnp.where(allowed[None, None], scores, -jnp.inf)
        row_max = lax.optimization_barrier(jnp.max(scores, axis=-1, keepdims=True))
        numer = jnp.exp(scores - row_max)
        row_sum = lax.optimization_barrier(jnp.sum(numer, axis=-1))
        weights = numer.astype(jnp.bfloat16)
        mixture = jnp.einsum('kgrn,nkd->rkgd', weights.astype(jnp.float32), all_values.astype(jnp.float32))
        return (mixture / jnp.transpose(row_sum, (2, 0, 1))[..., None]).astype(jnp.bfloat16)
    attended = lax.map(attend_rollout, (query_rolls, key_rolls, value_rolls, ancestors))
    attended = attended.reshape(LEAVES, QH * HD)
    return jnp.dot(attended, w_out, preferred_element_type=jnp.float32).astype(jnp.bfloat16)
```

```python
import math

import jax
import jax.numpy as jnp
import numpy as np
from jax import lax
from jax.experimental import pallas as pl
from jax.experimental.pallas import tpu as pltpu
from jax.sharding import PartitionSpec as P

QH = 32
KVH = 8
HD = 128
ROLL = 128
SEG_LEN = 256
DEPTH = 4
GROUP = QH // KVH
GRAN = 16

RING = 4


def y_shift(step):
    return [(y * 2 + c, ((y + step) % RING) * 2 + c) for y in range(RING) for c in range(2)]


SIBLING = [(h, h ^ 1) for h in range(2 * RING)]
UP = y_shift(1)
DOWN = y_shift(-1)


def send(x, pairs):
    return lax.ppermute(x, "head", pairs)


def params(mib):
    return pltpu.CompilerParams(vmem_limit_bytes=mib * 1024 * 1024)


def cost(flops, nbytes):
    return pl.CostEstimate(flops=int(flops), bytes_accessed=int(nbytes), transcendentals=0)


def index_table():
    rows = []
    for h in range(2 * RING):
        y, c = divmod(h, 2)
        row = []
        for other in (y, (y - 1) % RING, (y + 1) % RING, (y + 2) % RING):
            row += [2 * other + c, 2 * other + 1 - c]
        order = [(y + 2) % RING, (y + 1) % RING, (y - 1) % RING, y]
        row += [2 * t + c for t in order] + order
        row += [2 * t + 1 - c for t in range(RING)]
        rows.append(row)
    return np.asarray(rows, np.int32)


def spread_kernel(k_ref, v_ref, out_ref):
    out_ref[:, :, :GRAN, :] = pltpu.einshape("abcd->bacd", k_ref[...])
    out_ref[:, :, GRAN:, :] = pltpu.einshape("abcd->bacd", v_ref[...])


def spread(keys, values):
    segs = keys.shape[0] // SEG_LEN
    parts = SEG_LEN // GRAN
    step = 4
    view = (segs, parts, GRAN, HD)
    block = pl.BlockSpec((segs, step, GRAN, HD), lambda i: (0, i, 0, 0))
    return pl.pallas_call(
        spread_kernel,
        grid=(parts // step,),
        in_specs=[block, block],
        out_specs=pl.BlockSpec((step, segs, 2 * GRAN, HD), lambda i: (i, 0, 0, 0)),
        out_shape=jax.ShapeDtypeStruct((parts, segs, 2 * GRAN, HD), jnp.bfloat16),
        compiler_params=params(32),
        cost_estimate=cost(0, 4 * keys.size * 2),
    )(keys.reshape(view), values.reshape(view))


def pick_kernel(chain_ref, table_ref, out_ref):
    def body(n, carry):
        out_ref[n] = table_ref[jnp.maximum(chain_ref[n], 0)]
        return carry

    lax.fori_loop(0, out_ref.shape[0], body, 0, unroll=8)


def pick(chain, table):
    count = chain.shape[0]
    return pl.pallas_call(
        pick_kernel,
        grid_spec=pltpu.PrefetchScalarGridSpec(
            num_scalar_prefetch=1,
            grid=(1,),
            in_specs=[pl.BlockSpec(table.shape, lambda i, s: (0, 0, 0))],
            out_specs=pl.BlockSpec((count,) + table.shape[1:], lambda i, s: (0, 0, 0)),
        ),
        out_shape=jax.ShapeDtypeStruct((count,) + table.shape[1:], jnp.bfloat16),
        compiler_params=params(32),
        cost_estimate=cost(0, 2 * table.size * 2),
    )(chain, table)


def exchange(x):
    return lax.all_to_all(x, "seq", 0, 0, tiled=True)


def project_kernel(idx_ref, *refs):
    own, sib, *halves, wq, wk, wv, q_out, k_out, v_out, acc = refs
    step = pl.program_id(0)
    half = own.shape[0] // 2
    nq = wq.shape[1]
    nk = wk.shape[1]

    def add(rows, x, first):
        for w, lo, n in ((wq, 0, nq), (wk, nq, nk), (wv, nq + nk, nk)):
            d = jnp.dot(x, w[...], preferred_element_type=jnp.float32)
            if first:
                acc[rows, lo : lo + n] = d
            else:
                acc[rows, lo : lo + n] += d

    for s in range(8):

        @pl.when(step == s)
        def _():
            if s < 2:
                add(slice(None), (own, sib)[s][...], s == 0)
            else:
                top, bottom = halves[2 * (s - 2)], halves[2 * (s - 2) + 1]
                add(slice(0, half), top[...], False)
                add(slice(half, None), bottom[...], False)
            if s == 7:
                q_out[...] = acc[:, :nq].astype(jnp.bfloat16)
                k_out[...] = acc[:, nq : nq + nk].astype(jnp.bfloat16)
                v_out[...] = acc[:, nq + nk :].astype(jnp.bfloat16)


def project(idx, own, sib, halves, w_query, w_key, w_value):
    rows, depth = own.shape
    nq, nk = w_query.shape[1], w_key.shape[1]
    whole = lambda a: pl.BlockSpec(a.shape, lambda i, s: (0, 0))
    weight = lambda n: pl.BlockSpec((depth, n), lambda i, s: (s[i], 0))
    result = lambda n: pl.BlockSpec((rows, n), lambda i, s: (0, 0))
    return pl.pallas_call(
        project_kernel,
        grid_spec=pltpu.PrefetchScalarGridSpec(
            num_scalar_prefetch=1,
            grid=(8,),
            in_specs=[whole(a) for a in (own, sib, *halves)] + [weight(nq), weight(nk), weight(nk)],
            out_specs=[result(nq), result(nk), result(nk)],
            scratch_shapes=[pltpu.VMEM((rows, nq + 2 * nk), jnp.float32)],
        ),
        out_shape=[jax.ShapeDtypeStruct((rows, n), jnp.bfloat16) for n in (nq, nk, nk)],
        compiler_params=params(48),
        cost_estimate=cost(16 * rows * depth * (nq + 2 * nk), 16 * depth * (nq + 2 * nk + rows)),
    )(idx, own, sib, *halves, w_query, w_key, w_value)


def attend_kernel(chain_ref, len_ref, q_ref, k_ref, v_ref, far_ref, out_ref):
    base = (lax.axis_index("seq") * pl.num_programs(0) + pl.program_id(0)) * DEPTH
    inv_root = 1.0 / math.sqrt(HD)
    slot = lax.broadcasted_iota(jnp.int32, (1, SEG_LEN), 1)
    lives = []
    keys = []
    values = []
    for level in range(DEPTH):
        seg = chain_ref[base + level]
        live = jnp.where(seg >= 0, len_ref[jnp.maximum(seg, 0)], 0)
        lives.append(slot < live)
        keys.append(far_ref[:, level, :GRAN, :].reshape(SEG_LEN, HD))
        values.append(far_ref[:, level, GRAN:, :].reshape(SEG_LEN, HD))
    live = jnp.concatenate(lives, axis=1)
    keys = jnp.concatenate(keys, axis=0)
    values = jnp.concatenate(values, axis=0)
    own_keys = k_ref[...]
    own_values = v_ref[...]
    causal = lax.broadcasted_iota(jnp.int32, (ROLL, ROLL), 0) >= lax.broadcasted_iota(
        jnp.int32, (ROLL, ROLL), 1
    )
    nt = (((1,), (1,)), ((), ()))
    for g in range(GROUP):
        q = q_ref[:, g * HD : (g + 1) * HD]
        far = lax.dot_general(q, keys, nt, preferred_element_type=jnp.float32) * inv_root
        own = lax.dot_general(q, own_keys, nt, preferred_element_type=jnp.float32) * inv_root
        far = jnp.where(live, far, -jnp.inf)
        own = jnp.where(causal, own, -jnp.inf)
        m = jnp.maximum(
            jnp.max(far, axis=1, keepdims=True), jnp.max(own, axis=1, keepdims=True)
        )
        far = jnp.exp(far - m)
        own = jnp.exp(own - m)
        total = jnp.sum(far, axis=1, keepdims=True) + jnp.sum(own, axis=1, keepdims=True)
        mix = jnp.dot(far.astype(jnp.bfloat16), values, preferred_element_type=jnp.float32)
        mix += jnp.dot(own.astype(jnp.bfloat16), own_values, preferred_element_type=jnp.float32)
        out_ref[:, g * HD : (g + 1) * HD] = (mix / total).astype(jnp.bfloat16)


def attend(chain, lengths, q, k, v, far):
    rolls = q.shape[0] // ROLL
    row = lambda n: pl.BlockSpec((ROLL, n), lambda i, a, b: (i, 0))
    far_block = (far.shape[0], DEPTH, 2 * GRAN, HD)
    return pl.pallas_call(
        attend_kernel,
        grid_spec=pltpu.PrefetchScalarGridSpec(
            num_scalar_prefetch=2,
            grid=(rolls,),
            in_specs=[
                row(GROUP * HD),
                row(HD),
                row(HD),
                pl.BlockSpec(far_block, lambda i, a, b: (0, i, 0, 0)),
            ],
            out_specs=row(GROUP * HD),
        ),
        out_shape=jax.ShapeDtypeStruct(q.shape, jnp.bfloat16),
        compiler_params=params(48),
        cost_estimate=cost(4 * q.size * (DEPTH * SEG_LEN + ROLL), 2 * (2 * q.size + far.size)),
    )(chain, lengths, q, k, v, far)


def columns_kernel(idx_ref, w_ref, out_ref):
    out_ref[...] = w_ref[...]


def sibling_columns(idx, w_out):
    rows, cols = w_out.shape
    width = cols // (2 * RING)
    return pl.pallas_call(
        columns_kernel,
        grid_spec=pltpu.PrefetchScalarGridSpec(
            num_scalar_prefetch=1,
            grid=(RING,),
            in_specs=[pl.BlockSpec((rows, width), lambda j, s: (0, s[16 + j]))],
            out_specs=pl.BlockSpec((rows, width), lambda j, s: (0, j)),
        ),
        out_shape=jax.ShapeDtypeStruct((rows, RING * width), jnp.bfloat16),
        compiler_params=params(32),
        cost_estimate=cost(0, 2 * rows * cols),
    )(idx, w_out)


def chunk_kernel(idx_ref, a_ref, b_ref, wa_ref, wb_ref, *refs):
    *terms, out_ref = refs
    acc = jnp.dot(a_ref[...], wa_ref[...], preferred_element_type=jnp.float32)
    acc += jnp.dot(b_ref[...], wb_ref[...], preferred_element_type=jnp.float32)
    for t in terms:
        acc += t[...].astype(jnp.float32)
    out_ref[...] = acc.astype(out_ref.dtype)


def chunk(idx, which, part, parts, own, sib, w_own, w_sib, *terms):
    rows = own.shape[0] // parts
    depth = own.shape[1]
    width = w_own.shape[1] // (2 * RING)
    cut = 2
    tile = width // cut
    left = pl.BlockSpec((rows, depth), lambda j, s: (part, 0))
    term = pl.BlockSpec((rows, tile), lambda j, s: (0, j))
    return pl.pallas_call(
        chunk_kernel,
        grid_spec=pltpu.PrefetchScalarGridSpec(
            num_scalar_prefetch=1,
            grid=(cut,),
            in_specs=[
                left,
                left,
                pl.BlockSpec((depth, tile), lambda j, s: (0, s[8 + which] * cut + j)),
                pl.BlockSpec((depth, tile), lambda j, s: (0, s[12 + which] * cut + j)),
            ]
            + [term for _ in terms],
            out_specs=term,
        ),
        out_shape=jax.ShapeDtypeStruct((rows, width), jnp.bfloat16),
        compiler_params=params(32),
        cost_estimate=cost(4 * rows * depth * width, 4 * depth * width + 2 * rows * width),
    )(idx, own, sib, w_own, w_sib, *terms)


def per_device(
    hidden, w_query, w_key, w_value, w_out, prefix_keys, prefix_values, seg_lengths, ancestors
):
    head = lax.axis_index("head")
    idx = lax.dynamic_index_in_dim(jnp.asarray(index_table()), head, 0, keepdims=False)
    chain = ancestors.reshape(-1)
    half = hidden.shape[0] // 2

    top, bottom = hidden[:half], hidden[half:]
    low_top = send(top, UP)
    up_bottom = send(bottom, DOWN)
    low_bottom = send(bottom, UP)
    up_top = send(top, DOWN)
    sib = send(hidden, SIBLING)
    far_top = send(low_top, UP)
    far_bottom = send(up_bottom, DOWN)
    got = [low_top, low_bottom, up_top, up_bottom, far_top, far_bottom]
    twin = [send(x, SIBLING) for x in got]
    halves = []
    for n in range(3):
        halves += got[2 * n : 2 * n + 2] + twin[2 * n : 2 * n + 2]

    segs = spread(prefix_keys, prefix_values)
    table = exchange(segs).reshape(-1, 2 * GRAN, HD)
    wanted = pick(chain, table)
    far = exchange(wanted.reshape(segs.shape))

    w_sib = send(sibling_columns(idx, w_out), SIBLING)

    q, k, v = project(idx, hidden, sib, halves, w_query, w_key, w_value)
    own = attend(chain, seg_lengths, q, k, v, far)
    other = send(own, SIBLING)

    def piece(which, part, *terms):
        return chunk(idx, which, part, 2, own, other, w_out, w_sib, *terms)

    via_up = send(piece(0, 0), UP)
    via_down = send(piece(0, 1), DOWN)
    low_b = send(piece(1, 1), UP)
    up_t = send(piece(2, 0), DOWN)
    low_t = send(piece(1, 0, via_up), UP)
    up_b = send(piece(2, 1, via_down), DOWN)
    out_top = piece(3, 0, low_t, up_t)
    out_bottom = piece(3, 1, low_b, up_b)
    return jnp.concatenate([out_top, out_bottom], axis=0)


def solution(mesh):
    in_specs = (
        P("seq", "head"),
        P(None, "head"),
        P(None, "head"),
        P(None, "head"),
        P("head", None),
        P("seq", "head"),
        P("seq", "head"),
        P(),
        P(),
    )
    out_specs = P("seq", "head")
    return jax.shard_map(
        per_device, mesh=mesh, in_specs=in_specs, out_specs=out_specs, check_vma=False
    )
```

```python
import functools
import math

import jax
import jax.numpy as jnp
import numpy as np
from jax import lax
from jax.experimental import pallas as pl
from jax.experimental.pallas import tpu as pltpu
from jax.sharding import PartitionSpec as P

QH = 32
KVH = 8
HD = 128
ROLL = 128
SEG_LEN = 256
DEPTH = 4
GROUP = QH // KVH
GRAN = 16

RING = 4


def y_shift(step):
    return [(y * 2 + c, ((y + step) % RING) * 2 + c) for y in range(RING) for c in range(2)]


SIBLING = [(h, h ^ 1) for h in range(2 * RING)]
UP = y_shift(1)
DOWN = y_shift(-1)


def send(x, pairs):
    return lax.ppermute(x, "head", pairs)


def params(mib):
    return pltpu.CompilerParams(vmem_limit_bytes=mib * 1024 * 1024)


def cost(flops, nbytes):
    return pl.CostEstimate(flops=int(flops), bytes_accessed=int(nbytes), transcendentals=0)


def index_table():
    rows = []
    for h in range(2 * RING):
        y, c = divmod(h, 2)
        row = []
        for other in (y, (y - 1) % RING, (y + 1) % RING, (y + 2) % RING):
            row += [2 * other + c, 2 * other + 1 - c]
        order = [(y + 2) % RING, (y + 1) % RING, (y - 1) % RING, y]
        row += [2 * t + c for t in order]
        rows.append(row)
    return np.asarray(rows, np.int32)


def ordered_kernel(*refs):
    pass


def ordered(xs, after):
    anywhere = pl.BlockSpec(memory_space=pl.ANY)
    return pl.pallas_call(
        ordered_kernel,
        in_specs=[anywhere] * (len(xs) + 1),
        out_specs=[anywhere] * len(xs),
        out_shape=[jax.ShapeDtypeStruct(x.shape, x.dtype) for x in xs],
        input_output_aliases={n: n for n in range(len(xs))},
        cost_estimate=cost(0, 0),
    )(*xs, after)


def spread_kernel(k_ref, v_ref, out_ref):
    out_ref[:, :, :GRAN, :] = pltpu.einshape("abcd->bacd", k_ref[...])
    out_ref[:, :, GRAN:, :] = pltpu.einshape("abcd->bacd", v_ref[...])


def spread(keys, values):
    segs = keys.shape[0] // SEG_LEN
    parts = SEG_LEN // GRAN
    step = 4
    view = (segs, parts, GRAN, HD)
    block = pl.BlockSpec((segs, step, GRAN, HD), lambda i: (0, i, 0, 0))
    return pl.pallas_call(
        spread_kernel,
        grid=(parts // step,),
        in_specs=[block, block],
        out_specs=pl.BlockSpec((step, segs, 2 * GRAN, HD), lambda i: (i, 0, 0, 0)),
        out_shape=jax.ShapeDtypeStruct((parts, segs, 2 * GRAN, HD), jnp.bfloat16),
        compiler_params=params(60),
        cost_estimate=cost(0, 4 * keys.size * 2),
    )(keys.reshape(view), values.reshape(view))


def pick_kernel(chain_ref, table_ref, *refs):
    out_ref = refs[-1]
    devices, slots = out_ref.shape[:2]
    first = pl.program_id(0) * devices

    def body(d, carry):
        for n in range(slots):
            out_ref[d, n] = table_ref[jnp.maximum(chain_ref[(first + d) * slots + n], 0)]
        return carry

    lax.fori_loop(0, devices, body, 0)


def pick(chain, table, devices, after):
    slots = chain.shape[0] // devices
    steps = 4
    block = (devices // steps, slots) + table.shape[1:]
    return pl.pallas_call(
        pick_kernel,
        grid_spec=pltpu.PrefetchScalarGridSpec(
            num_scalar_prefetch=1,
            grid=(steps,),
            in_specs=[pl.BlockSpec(table.shape, lambda i, s: (0, 0, 0))]
            + [pl.BlockSpec(memory_space=pl.ANY) for _ in after],
            out_specs=pl.BlockSpec(block, lambda i, s: (i, 0, 0, 0)),
        ),
        out_shape=jax.ShapeDtypeStruct((devices, slots) + table.shape[1:], jnp.bfloat16),
        compiler_params=params(60),
        cost_estimate=cost(0, 4 * table.size),
    )(chain, table, *after)


def exchange(x):
    return lax.all_to_all(x, "seq", 0, 0, tiled=True)


def project_kernel(plan, skip, has_acc, is_last, idx_ref, *refs):
    count = sum(len(pieces) for pieces in plan)
    xs = refs[:count]
    wq, wk, wv = refs[count : count + 3]
    rest = refs[count + 3 :]
    start = rest[0] if has_acc else None
    outs = rest[skip + has_acc :]
    acc = outs[-1]
    step = pl.program_id(0)
    nq = wq.shape[1]
    nk = wk.shape[1]
    at = 0
    for s, pieces in enumerate(plan):
        mine = xs[at : at + len(pieces)]
        at += len(pieces)

        @pl.when(step == s)
        def _():
            for (lo, hi), x in zip(pieces, mine):
                for w, c, n in ((wq, 0, nq), (wk, nq, nk), (wv, nq + nk, nk)):
                    d = jnp.dot(x[...], w[...], preferred_element_type=jnp.float32)
                    if s == 0 and has_acc:
                        acc[lo:hi, c : c + n] = start[lo:hi, c : c + n] + d
                    elif s == 0:
                        acc[lo:hi, c : c + n] = d
                    else:
                        acc[lo:hi, c : c + n] += d
            if is_last and s == len(plan) - 1:
                outs[0][...] = acc[:, :nq].astype(jnp.bfloat16)
                outs[1][...] = acc[:, nq : nq + nk].astype(jnp.bfloat16)
                outs[2][...] = acc[:, nq + nk :].astype(jnp.bfloat16)


def project(idx, first, rows, plan, xs, weights, after, start=None, is_last=False):
    depth = xs[0].shape[1]
    nq, nk = weights[0].shape[1], weights[1].shape[1]
    whole = lambda a: pl.BlockSpec(a.shape, lambda i, s: (0, 0))
    weight = lambda n: pl.BlockSpec((depth, n), lambda i, s: (s[first + i], 0))
    result = lambda n: pl.BlockSpec((rows, n), lambda i, s: (0, 0))
    total = nq + 2 * nk
    if is_last:
        out_specs = [result(n) for n in (nq, nk, nk)]
        out_shape = [jax.ShapeDtypeStruct((rows, n), jnp.bfloat16) for n in (nq, nk, nk)]
        scratch = [pltpu.VMEM((rows, total), jnp.float32)]
    else:
        out_specs = result(total)
        out_shape = jax.ShapeDtypeStruct((rows, total), jnp.float32)
        scratch = []
    extra = [] if start is None else [start]
    steps = len(plan)
    return pl.pallas_call(
        functools.partial(project_kernel, plan, len(after), start is not None, is_last),
        grid_spec=pltpu.PrefetchScalarGridSpec(
            num_scalar_prefetch=1,
            grid=(steps,),
            in_specs=[whole(a) for a in xs]
            + [weight(nq), weight(nk), weight(nk)]
            + [whole(a) for a in extra]
            + [pl.BlockSpec(memory_space=pl.ANY) for _ in after],
            out_specs=out_specs,
            scratch_shapes=scratch,
        ),
        out_shape=out_shape,
        compiler_params=params(48),
        cost_estimate=cost(2 * steps * rows * depth * total, 2 * steps * depth * (total + rows)),
    )(idx, *xs, *weights, *extra, *after)


def attend_kernel(first, rolls, chain_ref, len_ref, q_ref, k_ref, v_ref, far_ref, *refs):
    out_ref = refs[-1]
    base = (lax.axis_index("seq") * rolls + first + pl.program_id(0)) * DEPTH
    scale = math.log2(math.e) / math.sqrt(HD)
    slot = lax.broadcasted_iota(jnp.int32, (1, SEG_LEN), 1)
    masks, keys, values = [], [], []
    for level in range(DEPTH):
        seg = chain_ref[base + level]
        live = jnp.where(seg >= 0, len_ref[jnp.maximum(seg, 0)], 0)
        masks.append(jnp.where(slot < live, 0.0, -jnp.inf))
        keys.append(far_ref[:, level, :GRAN, :].reshape(SEG_LEN, HD))
        values.append(far_ref[:, level, GRAN:, :].reshape(SEG_LEN, HD))
    mask = jnp.concatenate(masks, axis=1)
    keys = jnp.concatenate(keys, axis=0)
    values = jnp.concatenate(values, axis=0)
    row = lax.broadcasted_iota(jnp.int32, (ROLL, ROLL), 0)
    causal = jnp.where(row >= lax.broadcasted_iota(jnp.int32, (ROLL, ROLL), 1), 0.0, -jnp.inf)
    causal = jnp.concatenate([causal] * GROUP, axis=0)
    q = jnp.concatenate([q_ref[:, g * HD : (g + 1) * HD] for g in range(GROUP)], axis=0)
    nt = (((1,), (1,)), ((), ()))
    far = lax.dot_general(q, keys, nt, preferred_element_type=jnp.float32) + mask
    own = lax.dot_general(q, k_ref[...], nt, preferred_element_type=jnp.float32) + causal
    m = jnp.maximum(jnp.max(far, axis=1, keepdims=True), jnp.max(own, axis=1, keepdims=True))
    far = jnp.exp2((far - m) * scale)
    own = jnp.exp2((own - m) * scale)
    total = jnp.sum(far, axis=1, keepdims=True) + jnp.sum(own, axis=1, keepdims=True)
    mix = jnp.dot(far.astype(jnp.bfloat16), values, preferred_element_type=jnp.float32)
    mix += jnp.dot(own.astype(jnp.bfloat16), v_ref[...], preferred_element_type=jnp.float32)
    mix = (mix / total).astype(jnp.bfloat16)
    for g in range(GROUP):
        out_ref[:, g * HD : (g + 1) * HD] = mix[g * ROLL : (g + 1) * ROLL]


def attend(chain, lengths, q, k, v, far, part, parts, after):
    rolls = q.shape[0] // ROLL // parts
    row = lambda n: pl.BlockSpec((ROLL, n), lambda i, a, b: (part * rolls + i, 0))
    far_block = (far.shape[0], DEPTH, 2 * GRAN, HD)
    return pl.pallas_call(
        functools.partial(attend_kernel, part * rolls, parts * rolls),
        grid_spec=pltpu.PrefetchScalarGridSpec(
            num_scalar_prefetch=2,
            grid=(rolls,),
            in_specs=[
                row(GROUP * HD),
                row(HD),
                row(HD),
                pl.BlockSpec(far_block, lambda i, a, b: (0, i, 0, 0)),
            ]
            + [pl.BlockSpec(memory_space=pl.ANY) for _ in after],
            out_specs=pl.BlockSpec((ROLL, GROUP * HD), lambda i, a, b: (i, 0)),
        ),
        out_shape=jax.ShapeDtypeStruct((rolls * ROLL, GROUP * HD), jnp.bfloat16),
        compiler_params=params(48),
        cost_estimate=cost(
            4 * rolls * ROLL * GROUP * HD * (DEPTH * SEG_LEN + ROLL), 2 * (2 * q.size + far.size)
        ),
    )(chain, lengths, q, k, v, far, *after)


def terms_kernel(count, skip, outs, idx_ref, a_ref, b_ref, *refs):
    w_own, w_sib, results = refs[:count], refs[count : 2 * count], refs[2 * count + skip :]
    for k in range(count):
        acc = jnp.dot(a_ref[...], w_own[k][...], preferred_element_type=jnp.float32)
        acc += jnp.dot(b_ref[...], w_sib[k][...], preferred_element_type=jnp.float32)
        for (which, lo, hi, dtype), out_ref in zip(outs, results):
            if which == k:
                out_ref[...] = acc[lo:hi].astype(dtype)


def terms(idx, first, count, outs, after, own, sib, w_own, w_sib):
    rows, depth = own.shape
    width = w_own.shape[1] // (2 * RING)
    cut = 2
    tile = width // cut
    left = pl.BlockSpec((rows, depth), lambda j, s: (0, 0))
    weight = lambda k: pl.BlockSpec((depth, tile), lambda j, s: (0, s[8 + first + k] * cut + j))
    return pl.pallas_call(
        functools.partial(terms_kernel, count, len(after), outs),
        grid_spec=pltpu.PrefetchScalarGridSpec(
            num_scalar_prefetch=1,
            grid=(cut,),
            in_specs=[left, left]
            + [weight(k) for k in range(count)] * 2
            + [pl.BlockSpec(memory_space=pl.ANY) for _ in after],
            out_specs=[pl.BlockSpec((hi - lo, tile), lambda j, s: (0, j)) for _, lo, hi, _ in outs],
        ),
        out_shape=[jax.ShapeDtypeStruct((hi - lo, width), dtype) for _, lo, hi, dtype in outs],
        compiler_params=params(56),
        cost_estimate=cost(
            4 * count * rows * depth * width, 4 * count * depth * width + 4 * count * rows * width
        ),
    )(idx, own, sib, *([w_own] * count), *([w_sib] * count), *after)


def add_terms(x, *received):
    for r in received:
        x = x + r.astype(jnp.float32)
    return x.astype(jnp.bfloat16)


def summed(idx, own, sib, w_own, w_sib):
    rows = own.shape[0]
    half = rows // 2
    f32, b16 = jnp.float32, jnp.bfloat16
    args = (own, sib, w_own, w_sib)
    far_outs = ((0, 0, half, b16), (0, half, rows, b16))
    far_top, far_bottom = terms(idx, 0, 1, far_outs, [], *args)
    via_up = send(far_top, UP)
    via_down = send(far_bottom, DOWN)
    near_outs = ((0, 0, half, f32), (0, half, rows, b16), (1, 0, half, b16), (1, half, rows, f32))
    next_top, next_bottom, prev_top, prev_bottom = terms(idx, 1, 2, near_outs, [far_top], *args)
    low_bottom = send(next_bottom, UP)
    up_top = send(prev_top, DOWN)
    mine_outs = ((0, 0, half, f32), (0, half, rows, f32))
    mine_top, mine_bottom = terms(idx, 3, 1, mine_outs, [low_bottom, up_top], *args)
    low_top = send(add_terms(next_top, via_up), UP)
    up_bottom = send(add_terms(prev_bottom, via_down), DOWN)
    top = add_terms(mine_top, low_top, up_top)
    return jnp.concatenate([top, add_terms(mine_bottom, low_bottom, up_bottom)], axis=0)


def per_device(
    hidden, w_query, w_key, w_value, w_out, prefix_keys, prefix_values, seg_lengths, ancestors
):
    head = lax.axis_index("head")
    idx = lax.dynamic_index_in_dim(jnp.asarray(index_table()), head, 0, keepdims=False)
    chain = ancestors.reshape(-1)
    rows = hidden.shape[0]
    half = rows // 2
    devices = prefix_keys.shape[0] // SEG_LEN
    weights = (w_query, w_key, w_value)
    whole = ((0, rows),)
    split = ((0, half), (half, rows))

    low = send(hidden, UP)
    up = send(hidden, DOWN)
    sib = send(hidden, SIBLING)

    w_sib = send(w_out, SIBLING)

    segs = spread(prefix_keys, prefix_values)
    table = exchange(segs).reshape(-1, 2 * GRAN, HD)

    low_half, up_half = low[:half], up[half:]
    far = exchange(pick(chain, table, devices, [low_half, up_half]))

    near_blocks = [hidden, sib, low, send(low, SIBLING), up, send(up, SIBLING)]
    acc = project(idx, 0, rows, (whole,) * 6, near_blocks, weights, [])

    far_top, far_bottom = ordered([send(low_half, UP), send(up_half, DOWN)], acc)
    far_blocks = [far_top, far_bottom, send(far_top, SIBLING), send(far_bottom, SIBLING)]
    q, k, v = project(idx, 6, rows, (split,) * 2, far_blocks, weights, [], acc, True)

    own = attend(chain, seg_lengths, q, k, v, far, 0, 1, [])
    return summed(idx, own, send(own, SIBLING), w_out, w_sib)


def solution(mesh):
    in_specs = (
        P("seq", "head"),
        P(None, "head"),
        P(None, "head"),
        P(None, "head"),
        P("head", None),
        P("seq", "head"),
        P("seq", "head"),
        P(),
        P(),
    )
    out_specs = P("seq", "head")
    return jax.shard_map(
        per_device, mesh=mesh, in_specs=in_specs, out_specs=out_specs, check_vma=False
    )
```

```python
import functools
import math

import jax
import jax.numpy as jnp
import numpy as np
from jax import lax
from jax.experimental import pallas as pl
from jax.experimental.pallas import tpu as pltpu
from jax.sharding import PartitionSpec as P

QH = 32
KVH = 8
HD = 128
ROLL = 128
SEG_LEN = 256
DEPTH = 4
GROUP = QH // KVH
GRAN = 16

RING = 4


def y_shift(step):
    return [(y * 2 + c, ((y + step) % RING) * 2 + c) for y in range(RING) for c in range(2)]


SIBLING = [(h, h ^ 1) for h in range(2 * RING)]
UP = y_shift(1)
DOWN = y_shift(-1)


def send(x, pairs):
    return lax.ppermute(x, "head", pairs)


def params(mib):
    return pltpu.CompilerParams(vmem_limit_bytes=mib * 1024 * 1024)


def cost(flops, nbytes):
    return pl.CostEstimate(flops=int(flops), bytes_accessed=int(nbytes), transcendentals=0)


def index_table():
    rows = []
    for h in range(2 * RING):
        y, c = divmod(h, 2)
        row = []
        for other in (y, (y - 1) % RING, (y + 1) % RING, (y + 2) % RING):
            row += [2 * other + c, 2 * other + 1 - c]
        order = [(y + 2) % RING, (y + 1) % RING, (y - 1) % RING, y]
        row += [2 * t + c for t in order]
        rows.append(row)
    return np.asarray(rows, np.int32)


def ordered_kernel(*refs):
    pass


def ordered(xs, after):
    anywhere = pl.BlockSpec(memory_space=pl.ANY)
    return pl.pallas_call(
        ordered_kernel,
        in_specs=[anywhere] * (len(xs) + 1),
        out_specs=[anywhere] * len(xs),
        out_shape=[jax.ShapeDtypeStruct(x.shape, x.dtype) for x in xs],
        input_output_aliases={n: n for n in range(len(xs))},
        cost_estimate=cost(0, 0),
    )(*xs, after)


FIRST = 10
SECOND = 13
PARTS = SEG_LEN // GRAN
BATCH = 8


def table_kernel(chain_ref, len_ref, pack_ref, pick_ref, attend_ref, most_ref):
    f32, b16 = jnp.float32, jnp.bfloat16
    me = lax.axis_index("seq")
    chain = chain_ref[...]
    count = chain.shape[1]
    segs = len_ref.shape[1]
    iota = lambda shape, axis: lax.broadcasted_iota(jnp.int32, shape, axis)
    exact = lambda x, y: jnp.dot(x.astype(b16), y, preferred_element_type=f32)
    wants = jnp.where(iota((segs, count), 0) == chain, 1.0, 0.0).astype(b16)
    uses = lax.dot_general(
        jnp.ones((8, count), b16), wants, (((1,), (1,)), ((), ())), preferred_element_type=f32
    )[:1]
    lengths = len_ref[...].astype(f32)
    pieces = jnp.floor((lengths + (GRAN - 1)) * (1.0 / GRAN))
    live = exact(jnp.broadcast_to(lengths, (8, segs)), wants)
    row, col = iota((segs, segs), 0), iota((segs, segs), 1)
    earlier = jnp.where((row // PARTS == col // PARTS) & (row < col), 1.0, 0.0).astype(b16)
    mine = iota((segs, 128), 1)
    mine = jnp.where((iota((segs, 128), 0) == me * PARTS + mine) & (mine < PARTS), 1.0, 0.0)
    mine = mine.astype(b16)

    def number(level, held):
        device = iota((PARTS, segs), 0).astype(f32)
        piece = jnp.where(level % 2 == 1, (PARTS - 1) - device, device)
        counts = jnp.where(piece < held, 1.0, 0.0)
        before = exact(counts, earlier)
        return before, jnp.max(before + counts).astype(jnp.int32)

    def kept(x):
        return jnp.sum(jnp.where(iota(x.shape, 0) == me, x, 0.0), axis=0, keepdims=True)

    first, most_first = number(iota((1, segs), 1), jnp.where(uses > 0.0, pieces, 0.0))
    slot_pieces = jnp.floor((live[:1] + (GRAN - 1)) * (1.0 / GRAN))
    second, most_second = number(jnp.maximum(chain, 0), slot_pieces)
    source = jnp.maximum(chain, 0) // PARTS
    place = source * PARTS + kept(exact(first, wants)).astype(jnp.int32)
    to = kept(second).astype(jnp.int32)
    most = [jnp.full((1, segs), m, jnp.int32) for m in (most_first, most_second)]
    pick_ref[...] = jnp.concatenate([place, to] + most + [to] * 4, axis=0)
    pack_ref[:PARTS] = exact(first, mine).astype(jnp.int32)
    pack_ref[PARTS:] = jnp.full((8, 128), most_first, jnp.int32)
    attend_ref[:PARTS] = exact(second, mine).astype(jnp.int32)
    attend_ref[PARTS:] = exact(live, mine).astype(jnp.int32)
    most_ref[0] = most_first
    most_ref[1] = most_second


def number_pieces(chain, lengths):
    vmem = pl.BlockSpec(memory_space=pltpu.VMEM)
    own = jax.ShapeDtypeStruct((PARTS + 8, 128), jnp.int32)
    return pl.pallas_call(
        table_kernel,
        out_specs=[vmem, vmem, vmem, pl.BlockSpec(memory_space=pltpu.SMEM)],
        out_shape=[
            own,
            jax.ShapeDtypeStruct((8, chain.size), jnp.int32),
            own,
            jax.ShapeDtypeStruct((2,), jnp.int32),
        ],
        compiler_params=params(32),
        cost_estimate=cost(0, 0),
    )(chain.reshape(1, -1), lengths.reshape(1, -1))


def pack_kernel(lo, hi, first_ref, k0_ref, k1_ref, v0_ref, v1_ref, out_ref):
    pairs, _, step = k0_ref.shape[:3]
    block = pl.program_id(0) * step

    def piece_of(j, i):
        odd = j % 2
        piece = step - 1 - i if odd else i
        return (k0_ref, k1_ref)[odd][j // 2, 0, piece], (v0_ref, v1_ref)[odd][j // 2, 0, piece]

    def put(i, at, pair):
        out_ref[i, at, :GRAN] = pair[0]
        out_ref[i, at, GRAN:] = pair[1]

    def guarded(i, carry):
        for j in range(2 * pairs):
            at = first_ref[block + i, j]
            pl.when((at >= lo) & (at < hi))(lambda: put(i, at - lo, piece_of(j, i)))
        return carry

    def plain(i, carry):
        for j0 in range(0, 2 * pairs, BATCH):
            batch = range(j0, j0 + BATCH)
            at = [first_ref[block + i, j] for j in batch]
            for a, pair in zip(at, [piece_of(j, i) for j in batch]):
                put(i, a, pair)
        return carry

    most = first_ref[PARTS, 0]
    spare = (most < hi) if lo == 0 else (most < 0)
    pl.when(spare)(lambda: lax.fori_loop(0, step, plain, None))
    pl.when(jnp.logical_not(spare))(lambda: lax.fori_loop(0, step, guarded, None))


def pack(lo, hi, first, keys, values):
    segs = keys.shape[0] // SEG_LEN
    steps = 4
    step = PARTS // steps
    view = (segs // 2, 2, PARTS, GRAN, HD)
    block = (segs // 2, 1, step, GRAN, HD)
    even = pl.BlockSpec(block, lambda i, *s: (0, 0, i, 0, 0))
    odd = pl.BlockSpec(block, lambda i, *s: (0, 1, steps - 1 - i, 0, 0))
    shape = (PARTS, hi - lo, 2 * GRAN, HD)
    keys, values = keys.reshape(view), values.reshape(view)
    return pl.pallas_call(
        functools.partial(pack_kernel, lo, hi),
        grid_spec=pltpu.PrefetchScalarGridSpec(
            num_scalar_prefetch=1,
            grid=(steps,),
            in_specs=[even, odd, even, odd],
            out_specs=pl.BlockSpec((step,) + shape[1:], lambda i, *s: (i, 0, 0, 0)),
        ),
        out_shape=jax.ShapeDtypeStruct(shape, jnp.bfloat16),
        compiler_params=params(60),
        cost_estimate=cost(0, 4 * keys.size * 2),
    )(first, keys, keys, values, values)


def pick_kernel(lo, hi, split, slot_ref, *refs):
    table_ref, out_ref = refs[0], refs[-1]
    devices = out_ref.shape[0]
    slots = slot_ref.shape[1] // PARTS
    base = pl.program_id(0) * devices

    def piece_of(place):
        source, at = place // PARTS, place % PARTS
        piece = table_ref[source, jnp.minimum(at, FIRST - 1)]
        if split:
            rest = refs[1][source, jnp.maximum(at - FIRST, 0)]
            piece = jnp.where(at < FIRST, piece, rest)
        return piece

    def put(d, to, piece):
        out_ref[d, to] = piece

    def guarded(d, carry):
        for n in range(slots):
            slot = (base + d) * slots + n
            to = slot_ref[1, slot]
            pl.when((to >= lo) & (to < hi))(lambda: put(d, to - lo, piece_of(slot_ref[0, slot])))
        return carry

    def plain(d, carry):
        for n0 in range(0, slots, BATCH):
            batch = [(base + d) * slots + n for n in range(n0, n0 + BATCH)]
            to = [slot_ref[1, slot] for slot in batch]
            for t, piece in zip(to, [piece_of(slot_ref[0, slot]) for slot in batch]):
                put(d, t, piece)
        return carry

    most = slot_ref[3, 0]
    spare = (most < hi) if lo == 0 else (most < 0)
    pl.when(spare)(lambda: lax.fori_loop(0, devices, plain, None))
    pl.when(jnp.logical_not(spare))(lambda: lax.fori_loop(0, devices, guarded, None))


def pick(lo, hi, slots, tables, after):
    steps = 4
    shape = (PARTS, hi - lo, 2 * GRAN, HD)
    return pl.pallas_call(
        functools.partial(pick_kernel, lo, hi, len(tables) > 1),
        grid_spec=pltpu.PrefetchScalarGridSpec(
            num_scalar_prefetch=1,
            grid=(steps,),
            in_specs=[pl.BlockSpec(t.shape, lambda i, *s: (0, 0, 0, 0)) for t in tables]
            + [pl.BlockSpec(memory_space=pl.ANY) for _ in after],
            out_specs=pl.BlockSpec((PARTS // steps,) + shape[1:], lambda i, *s: (i, 0, 0, 0)),
        ),
        out_shape=jax.ShapeDtypeStruct(shape, jnp.bfloat16),
        compiler_params=params(60),
        cost_estimate=cost(0, 4 * tables[0].size),
    )(slots, *tables, *after)


def exchange(x):
    return lax.all_to_all(x, "seq", 0, 0, tiled=True)


def project_kernel(plan, skip, has_acc, is_last, idx_ref, *refs):
    count = sum(len(pieces) for pieces in plan)
    xs = refs[:count]
    wq, wk, wv = refs[count : count + 3]
    rest = refs[count + 3 :]
    start = rest[0] if has_acc else None
    outs = rest[skip + has_acc :]
    acc = outs[-1]
    step = pl.program_id(0)
    nq = wq.shape[1]
    nk = wk.shape[1]
    at = 0
    for s, pieces in enumerate(plan):
        mine = xs[at : at + len(pieces)]
        at += len(pieces)

        @pl.when(step == s)
        def _():
            for (lo, hi), x in zip(pieces, mine):
                for w, c, n in ((wq, 0, nq), (wk, nq, nk), (wv, nq + nk, nk)):
                    d = jnp.dot(x[...], w[...], preferred_element_type=jnp.float32)
                    if s == 0 and has_acc:
                        acc[lo:hi, c : c + n] = start[lo:hi, c : c + n] + d
                    elif s == 0:
                        acc[lo:hi, c : c + n] = d
                    else:
                        acc[lo:hi, c : c + n] += d
            if is_last and s == len(plan) - 1:
                outs[0][...] = acc[:, :nq].astype(jnp.bfloat16)
                outs[1][...] = acc[:, nq : nq + nk].astype(jnp.bfloat16)
                outs[2][...] = acc[:, nq + nk :].astype(jnp.bfloat16)


def project(idx, first, rows, plan, xs, weights, after, start=None, is_last=False):
    depth = xs[0].shape[1]
    nq, nk = weights[0].shape[1], weights[1].shape[1]
    whole = lambda a: pl.BlockSpec(a.shape, lambda i, s: (0, 0))
    weight = lambda n: pl.BlockSpec((depth, n), lambda i, s: (s[first + i], 0))
    result = lambda n: pl.BlockSpec((rows, n), lambda i, s: (0, 0))
    total = nq + 2 * nk
    if is_last:
        out_specs = [result(n) for n in (nq, nk, nk)]
        out_shape = [jax.ShapeDtypeStruct((rows, n), jnp.bfloat16) for n in (nq, nk, nk)]
        scratch = [pltpu.VMEM((rows, total), jnp.float32)]
    else:
        out_specs = result(total)
        out_shape = jax.ShapeDtypeStruct((rows, total), jnp.float32)
        scratch = []
    extra = [] if start is None else [start]
    steps = len(plan)
    return pl.pallas_call(
        functools.partial(project_kernel, plan, len(after), start is not None, is_last),
        grid_spec=pltpu.PrefetchScalarGridSpec(
            num_scalar_prefetch=1,
            grid=(steps,),
            in_specs=[whole(a) for a in xs]
            + [weight(nq), weight(nk), weight(nk)]
            + [whole(a) for a in extra]
            + [pl.BlockSpec(memory_space=pl.ANY) for _ in after],
            out_specs=out_specs,
            scratch_shapes=scratch,
        ),
        out_shape=out_shape,
        compiler_params=params(48),
        cost_estimate=cost(2 * steps * rows * depth * total, 2 * steps * depth * (total + rows)),
    )(idx, *xs, *weights, *extra, *after)


HEADS = 2


def attend_kernel(slot_ref, q_ref, k_ref, v_ref, *refs):
    *tables, out_ref, keys, values = refs
    roll = pl.program_id(0)
    scale = math.log2(math.e) / math.sqrt(HD)
    slot = lax.broadcasted_iota(jnp.int32, (1, SEG_LEN), 1)
    masks = []
    for level in range(DEPTH):
        at = roll * DEPTH + level
        live = slot_ref[PARTS, at]
        row = slot
        if level % 2:
            row = (PARTS - 1 - slot // GRAN) * GRAN + slot % GRAN
        masks.append(jnp.where(row < live, 0.0, -jnp.inf))
        pieces = []
        for i in range(PARTS):
            to = slot_ref[i, at]
            piece = tables[0][i, jnp.minimum(to, SECOND - 1)]
            if len(tables) > 1:
                rest = tables[1][i, jnp.maximum(to - SECOND, 0)]
                piece = jnp.where(to < SECOND, piece, rest)
            pieces.append(piece)
        lo = level * SEG_LEN
        keys[lo : lo + SEG_LEN] = jnp.concatenate([p[:GRAN] for p in pieces], axis=0)
        values[lo : lo + SEG_LEN] = jnp.concatenate([p[GRAN:] for p in pieces], axis=0)
    mask = jnp.concatenate(masks, axis=1)
    row = lax.broadcasted_iota(jnp.int32, (ROLL, ROLL), 0)
    causal = jnp.where(row >= lax.broadcasted_iota(jnp.int32, (ROLL, ROLL), 1), 0.0, -jnp.inf)
    causal = jnp.concatenate([causal] * HEADS, axis=0)
    nt = (((1,), (1,)), ((), ()))
    for g0 in range(0, GROUP, HEADS):
        heads = range(g0, g0 + HEADS)
        q = jnp.concatenate([q_ref[:, g * HD : (g + 1) * HD] for g in heads], axis=0)
        far = lax.dot_general(q, keys[...], nt, preferred_element_type=jnp.float32) + mask
        own = lax.dot_general(q, k_ref[...], nt, preferred_element_type=jnp.float32) + causal
        m = jnp.maximum(jnp.max(far, axis=1, keepdims=True), jnp.max(own, axis=1, keepdims=True))
        far = jnp.exp2((far - m) * scale)
        own = jnp.exp2((own - m) * scale)
        total = jnp.sum(far, axis=1, keepdims=True) + jnp.sum(own, axis=1, keepdims=True)
        mix = jnp.dot(far.astype(jnp.bfloat16), values[...], preferred_element_type=jnp.float32)
        mix += jnp.dot(own.astype(jnp.bfloat16), v_ref[...], preferred_element_type=jnp.float32)
        mix = (mix / total).astype(jnp.bfloat16)
        for n, g in enumerate(heads):
            out_ref[:, g * HD : (g + 1) * HD] = mix[n * ROLL : (n + 1) * ROLL]


def attend(slots, q, k, v, tables):
    rolls = q.shape[0] // ROLL
    row = lambda n: pl.BlockSpec((ROLL, n), lambda i, *s: (i, 0))
    return pl.pallas_call(
        attend_kernel,
        grid_spec=pltpu.PrefetchScalarGridSpec(
            num_scalar_prefetch=1,
            grid=(rolls,),
            in_specs=[row(GROUP * HD), row(HD), row(HD)]
            + [pl.BlockSpec(t.shape, lambda i, *s: (0, 0, 0, 0)) for t in tables],
            out_specs=row(GROUP * HD),
            scratch_shapes=[
                pltpu.VMEM((DEPTH * SEG_LEN, HD), jnp.bfloat16),
                pltpu.VMEM((DEPTH * SEG_LEN, HD), jnp.bfloat16),
            ],
        ),
        out_shape=jax.ShapeDtypeStruct(q.shape, jnp.bfloat16),
        compiler_params=params(48),
        cost_estimate=cost(
            4 * q.size * (DEPTH * SEG_LEN + ROLL), 4 * (q.size + tables[0].size)
        ),
    )(slots, q, k, v, *tables)


def terms_kernel(count, skip, outs, idx_ref, a_ref, b_ref, *refs):
    w_own, w_sib, results = refs[:count], refs[count : 2 * count], refs[2 * count + skip :]
    for k in range(count):
        acc = jnp.dot(a_ref[...], w_own[k][...], preferred_element_type=jnp.float32)
        acc += jnp.dot(b_ref[...], w_sib[k][...], preferred_element_type=jnp.float32)
        for (which, lo, hi, dtype), out_ref in zip(outs, results):
            if which == k:
                out_ref[...] = acc[lo:hi].astype(dtype)


def terms(idx, first, count, outs, after, own, sib, w_own, w_sib):
    rows, depth = own.shape
    width = w_own.shape[1] // (2 * RING)
    cut = 2
    tile = width // cut
    left = pl.BlockSpec((rows, depth), lambda j, s: (0, 0))
    weight = lambda k: pl.BlockSpec((depth, tile), lambda j, s: (0, s[8 + first + k] * cut + j))
    return pl.pallas_call(
        functools.partial(terms_kernel, count, len(after), outs),
        grid_spec=pltpu.PrefetchScalarGridSpec(
            num_scalar_prefetch=1,
            grid=(cut,),
            in_specs=[left, left]
            + [weight(k) for k in range(count)] * 2
            + [pl.BlockSpec(memory_space=pl.ANY) for _ in after],
            out_specs=[pl.BlockSpec((hi - lo, tile), lambda j, s: (0, j)) for _, lo, hi, _ in outs],
        ),
        out_shape=[jax.ShapeDtypeStruct((hi - lo, width), dtype) for _, lo, hi, dtype in outs],
        compiler_params=params(56),
        cost_estimate=cost(
            4 * count * rows * depth * width, 4 * count * depth * width + 4 * count * rows * width
        ),
    )(idx, own, sib, *([w_own] * count), *([w_sib] * count), *after)


def add_terms(x, *received):
    for r in received:
        x = x + r.astype(jnp.float32)
    return x.astype(jnp.bfloat16)


def summed(idx, own, sib, w_own, w_sib):
    rows = own.shape[0]
    half = rows // 2
    f32, b16 = jnp.float32, jnp.bfloat16
    args = (own, sib, w_own, w_sib)
    far_outs = ((0, 0, half, b16), (0, half, rows, b16))
    far_top, far_bottom = terms(idx, 0, 1, far_outs, [], *args)
    via_up = send(far_top, UP)
    via_down = send(far_bottom, DOWN)
    near_outs = ((0, 0, half, f32), (0, half, rows, b16), (1, 0, half, b16), (1, half, rows, f32))
    next_top, next_bottom, prev_top, prev_bottom = terms(idx, 1, 2, near_outs, [far_top], *args)
    low_bottom = send(next_bottom, UP)
    up_top = send(prev_top, DOWN)
    mine_outs = ((0, 0, half, f32), (0, half, rows, f32))
    mine_top, mine_bottom = terms(idx, 3, 1, mine_outs, [low_bottom, up_top], *args)
    low_top = send(add_terms(next_top, via_up), UP)
    up_bottom = send(add_terms(prev_bottom, via_down), DOWN)
    top = add_terms(mine_top, low_top, up_top)
    return jnp.concatenate([top, add_terms(mine_bottom, low_bottom, up_bottom)], axis=0)


def per_device(
    hidden, w_query, w_key, w_value, w_out, prefix_keys, prefix_values, seg_lengths, ancestors
):
    head = lax.axis_index("head")
    idx = lax.dynamic_index_in_dim(jnp.asarray(index_table()), head, 0, keepdims=False)
    chain = ancestors.reshape(-1)
    rows = hidden.shape[0]
    half = rows // 2
    weights = (w_query, w_key, w_value)
    whole = ((0, rows),)
    split = ((0, half), (half, rows))

    low = send(hidden, UP)
    up = send(hidden, DOWN)
    sib = send(hidden, SIBLING)

    w_sib = send(w_out, SIBLING)

    for_pack, for_pick, for_attend, most = number_pieces(chain, seg_lengths)
    table = exchange(pack(0, FIRST, for_pack, prefix_keys, prefix_values))

    acc = project(idx, 0, rows, (whole,) * 2, [hidden, sib], weights, [low])
    low_half, up_half = low[:half], up[half:]

    def rest():
        return exchange(pack(FIRST, PARTS, for_pack, prefix_keys, prefix_values))

    def pick_all(lo, hi, tables):
        return pick(lo, hi, for_pick, tables, [acc])

    picked = lax.cond(
        most[0] > FIRST,
        lambda: pick_all(0, SECOND, [table, rest()]),
        lambda: pick_all(0, SECOND, [table]),
    )
    far = exchange(picked)

    near_blocks = [low, send(low, SIBLING), up, send(up, SIBLING)]
    acc = project(idx, 2, rows, (whole,) * 4, near_blocks, weights, [], acc)

    far_top, far_bottom = ordered([send(low_half, UP), send(up_half, DOWN)], acc)
    far_blocks = [far_top, far_bottom, send(far_top, SIBLING), send(far_bottom, SIBLING)]
    q, k, v = project(idx, 6, rows, (split,) * 2, far_blocks, weights, [], acc, True)

    def attend_rest():
        far_rest = exchange(pick_all(SECOND, PARTS, [table, rest()]))
        return attend(for_attend, q, k, v, [far, far_rest])

    def attend_all():
        return attend(for_attend, q, k, v, [far])

    own = lax.cond(most[1] > SECOND, attend_rest, attend_all)
    return summed(idx, own, send(own, SIBLING), w_out, w_sib)


def solution(mesh):
    in_specs = (
        P("seq", "head"),
        P(None, "head"),
        P(None, "head"),
        P(None, "head"),
        P("head", None),
        P("seq", "head"),
        P("seq", "head"),
        P(),
        P(),
    )
    out_specs = P("seq", "head")
    return jax.shard_map(
        per_device, mesh=mesh, in_specs=in_specs, out_specs=out_specs, check_vma=False
    )
```

```python
import functools
import math

import jax
import jax.numpy as jnp
import numpy as np
from jax import lax
from jax.experimental import pallas as pl
from jax.experimental.pallas import tpu as pltpu
from jax.sharding import PartitionSpec as P

QH = 32
KVH = 8
HD = 128
ROLL = 128
SEG_LEN = 256
DEPTH = 4
GROUP = QH // KVH
GRAN = 16

RING = 4


def y_shift(step):
    return [(y * 2 + c, ((y + step) % RING) * 2 + c) for y in range(RING) for c in range(2)]


SIBLING = [(h, h ^ 1) for h in range(2 * RING)]
UP = y_shift(1)
DOWN = y_shift(-1)


def send(x, pairs):
    return lax.ppermute(x, "head", pairs)


def params(mib):
    return pltpu.CompilerParams(vmem_limit_bytes=mib * 1024 * 1024)


def cost(flops, nbytes):
    return pl.CostEstimate(flops=int(flops), bytes_accessed=int(nbytes), transcendentals=0)


def index_table():
    rows = []
    for h in range(2 * RING):
        y, c = divmod(h, 2)
        row = []
        for other in (y, (y - 1) % RING, (y + 1) % RING, (y + 2) % RING):
            row += [2 * other + c, 2 * other + 1 - c]
        order = [(y + 2) % RING, (y + 1) % RING, (y - 1) % RING, y]
        row += [2 * t + c for t in order]
        rows.append(row)
    return np.asarray(rows, np.int32)


def ordered_kernel(*refs):
    pass


def ordered(xs, after):
    anywhere = pl.BlockSpec(memory_space=pl.ANY)
    return pl.pallas_call(
        ordered_kernel,
        in_specs=[anywhere] * (len(xs) + 1),
        out_specs=[anywhere] * len(xs),
        out_shape=[jax.ShapeDtypeStruct(x.shape, x.dtype) for x in xs],
        input_output_aliases={n: n for n in range(len(xs))},
        cost_estimate=cost(0, 0),
    )(*xs, after)


FIRST = 10
SECOND = 13
PARTS = SEG_LEN // GRAN
STEPS = 4
BATCH = 8


def table_kernel(chain_ref, len_ref, pack_ref, pick_ref, attend_ref, most_ref):
    f32, b16 = jnp.float32, jnp.bfloat16
    me = lax.axis_index("seq")
    chain = chain_ref[...]
    count = chain.shape[1]
    segs = len_ref.shape[1]
    iota = lambda shape, axis: lax.broadcasted_iota(jnp.int32, shape, axis)
    exact = lambda x, y: jnp.dot(x.astype(b16), y, preferred_element_type=f32)
    wants = jnp.where(iota((segs, count), 0) == chain, 1.0, 0.0).astype(b16)
    uses = lax.dot_general(
        jnp.ones((8, count), b16), wants, (((1,), (1,)), ((), ())), preferred_element_type=f32
    )[:1]
    lengths = len_ref[...].astype(f32)
    pieces = jnp.floor((lengths + (GRAN - 1)) * (1.0 / GRAN))
    live = exact(jnp.broadcast_to(lengths, (8, segs)), wants)
    row, col = iota((segs, segs), 0), iota((segs, segs), 1)
    earlier = jnp.where((row // PARTS == col // PARTS) & (row < col), 1.0, 0.0).astype(b16)
    mine = iota((segs, 128), 1)
    mine = jnp.where((iota((segs, 128), 0) == me * PARTS + mine) & (mine < PARTS), 1.0, 0.0)
    mine = mine.astype(b16)

    def number(level, held):
        device = iota((PARTS, segs), 0).astype(f32)
        piece = jnp.where(level % 2 == 1, (PARTS - 1) - device, device)
        counts = jnp.where(piece < held, 1.0, 0.0)
        before = exact(counts, earlier)
        return before, jnp.max(before + counts).astype(jnp.int32)

    def kept(x):
        return jnp.sum(jnp.where(iota(x.shape, 0) == me, x, 0.0), axis=0, keepdims=True)

    first, most_first = number(iota((1, segs), 1), jnp.where(uses > 0.0, pieces, 0.0))
    slot_pieces = jnp.floor((live[:1] + (GRAN - 1)) * (1.0 / GRAN))
    second, most_second = number(jnp.maximum(chain, 0), slot_pieces)
    source = jnp.maximum(chain, 0) // PARTS
    place = source * PARTS + kept(exact(first, wants)).astype(jnp.int32)
    to = kept(second).astype(jnp.int32)
    most = [jnp.full((1, segs), m, jnp.int32) for m in (most_first, most_second)]
    at = place - source * PARTS
    from_row = source * FIRST + jnp.minimum(at, FIRST - 1)
    to_row = (iota((1, segs), 1) // PARTS) % (PARTS // STEPS) * SECOND + to
    pick_ref[...] = jnp.concatenate([place, to] + most + [from_row, to_row] * 2, axis=0)
    pack_ref[:PARTS] = exact(first, mine).astype(jnp.int32)
    pack_ref[PARTS:] = jnp.full((8, 128), most_first, jnp.int32)
    attend_ref[:PARTS] = exact(second, mine).astype(jnp.int32)
    attend_ref[PARTS:] = exact(live, mine).astype(jnp.int32)
    most_ref[0] = most_first
    most_ref[1] = most_second


def number_pieces(chain, lengths):
    vmem = pl.BlockSpec(memory_space=pltpu.VMEM)
    own = jax.ShapeDtypeStruct((PARTS + 8, 128), jnp.int32)
    return pl.pallas_call(
        table_kernel,
        out_specs=[vmem, vmem, vmem, pl.BlockSpec(memory_space=pltpu.SMEM)],
        out_shape=[
            own,
            jax.ShapeDtypeStruct((8, chain.size), jnp.int32),
            own,
            jax.ShapeDtypeStruct((2,), jnp.int32),
        ],
        compiler_params=params(32),
        cost_estimate=cost(0, 0),
    )(chain.reshape(1, -1), lengths.reshape(1, -1))


def pack_kernel(lo, hi, first_ref, k0_ref, k1_ref, v0_ref, v1_ref, out_ref):
    pairs, _, step = k0_ref.shape[:3]
    block = pl.program_id(0) * step

    def piece_of(j, i):
        odd = j % 2
        piece = step - 1 - i if odd else i
        return (k0_ref, k1_ref)[odd][j // 2, 0, piece], (v0_ref, v1_ref)[odd][j // 2, 0, piece]

    def put(i, at, pair):
        out_ref[i, at, :GRAN] = pair[0]
        out_ref[i, at, GRAN:] = pair[1]

    def guarded(i, carry):
        for j in range(2 * pairs):
            at = first_ref[block + i, j]
            pl.when((at >= lo) & (at < hi))(lambda: put(i, at - lo, piece_of(j, i)))
        return carry

    def plain():
        for i in range(step):
            for j0 in range(0, 2 * pairs, BATCH):
                batch = range(j0, j0 + BATCH)
                at = [first_ref[block + i, j] for j in batch]
                for a, pair in zip(at, [piece_of(j, i) for j in batch]):
                    put(i, a, pair)

    most = first_ref[PARTS, 0]
    if lo == 0:
        pl.when(most < hi)(plain)
        pl.when(most >= hi)(lambda: lax.fori_loop(0, step, guarded, None))
    else:
        lax.fori_loop(0, step, guarded, None)


def pack(lo, hi, first, keys, values):
    segs = keys.shape[0] // SEG_LEN
    steps = 4
    step = PARTS // steps
    view = (segs // 2, 2, PARTS, GRAN, HD)
    block = (segs // 2, 1, step, GRAN, HD)
    even = pl.BlockSpec(block, lambda i, *s: (0, 0, i, 0, 0))
    odd = pl.BlockSpec(block, lambda i, *s: (0, 1, steps - 1 - i, 0, 0))
    shape = (PARTS, hi - lo, 2 * GRAN, HD)
    keys, values = keys.reshape(view), values.reshape(view)
    return pl.pallas_call(
        functools.partial(pack_kernel, lo, hi),
        grid_spec=pltpu.PrefetchScalarGridSpec(
            num_scalar_prefetch=1,
            grid=(steps,),
            in_specs=[even, odd, even, odd],
            out_specs=pl.BlockSpec((step,) + shape[1:], lambda i, *s: (i, 0, 0, 0)),
        ),
        out_shape=jax.ShapeDtypeStruct(shape, jnp.bfloat16),
        compiler_params=params(60),
        cost_estimate=cost(0, 4 * keys.size * 2),
    )(first, keys, keys, values, values)


def pick_kernel(lo, hi, split, slot_ref, *refs):
    table_ref, out_ref = refs[0], refs[-1]
    devices = out_ref.shape[0]
    slots = slot_ref.shape[1] // PARTS
    base = pl.program_id(0) * devices

    def piece_of(place):
        source, at = place // PARTS, place % PARTS
        piece = table_ref[source, jnp.minimum(at, FIRST - 1)]
        if split:
            rest = refs[1][source, jnp.maximum(at - FIRST, 0)]
            piece = jnp.where(at < FIRST, piece, rest)
        return piece

    def put(d, to, piece):
        out_ref[d, to] = piece

    def guarded(d, carry):
        for n in range(slots):
            slot = (base + d) * slots + n
            to = slot_ref[1, slot]
            pl.when((to >= lo) & (to < hi))(lambda: put(d, to - lo, piece_of(slot_ref[0, slot])))
        return carry

    def plain():
        flat = table_ref.reshape(PARTS * FIRST, 2 * GRAN, HD)
        out = out_ref.reshape(devices * (hi - lo), 2 * GRAN, HD)
        for n0 in range(0, devices * slots, BATCH):
            batch = [base * slots + n for n in range(n0, n0 + BATCH)]
            pieces = [flat[slot_ref[4, slot]] for slot in batch]
            for slot, piece in zip(batch, pieces):
                out[slot_ref[5, slot]] = piece

    most = slot_ref[3, 0]
    if lo == 0 and not split:
        pl.when(most < hi)(plain)
        pl.when(most >= hi)(lambda: lax.fori_loop(0, devices, guarded, None))
    else:
        lax.fori_loop(0, devices, guarded, None)


def pick(lo, hi, slots, tables, after):
    steps = STEPS
    shape = (PARTS, hi - lo, 2 * GRAN, HD)
    return pl.pallas_call(
        functools.partial(pick_kernel, lo, hi, len(tables) > 1),
        grid_spec=pltpu.PrefetchScalarGridSpec(
            num_scalar_prefetch=1,
            grid=(steps,),
            in_specs=[pl.BlockSpec(t.shape, lambda i, *s: (0, 0, 0, 0)) for t in tables]
            + [pl.BlockSpec(memory_space=pl.ANY) for _ in after],
            out_specs=pl.BlockSpec((PARTS // steps,) + shape[1:], lambda i, *s: (i, 0, 0, 0)),
        ),
        out_shape=jax.ShapeDtypeStruct(shape, jnp.bfloat16),
        compiler_params=params(60),
        cost_estimate=cost(0, 4 * tables[0].size),
    )(slots, *tables, *after)


def exchange(x):
    return lax.all_to_all(x, "seq", 0, 0, tiled=True)


def project_kernel(plan, skip, has_acc, is_last, idx_ref, *refs):
    count = sum(len(pieces) for pieces in plan)
    xs = refs[:count]
    wq, wk, wv = refs[count : count + 3]
    rest = refs[count + 3 :]
    start = rest[0] if has_acc else None
    outs = rest[skip + has_acc :]
    acc = outs[-1]
    step = pl.program_id(0)
    nq = wq.shape[1]
    nk = wk.shape[1]
    at = 0
    for s, pieces in enumerate(plan):
        mine = xs[at : at + len(pieces)]
        at += len(pieces)

        @pl.when(step == s)
        def _():
            for (lo, hi), x in zip(pieces, mine):
                for w, c, n in ((wq, 0, nq), (wk, nq, nk), (wv, nq + nk, nk)):
                    d = jnp.dot(x[...], w[...], preferred_element_type=jnp.float32)
                    if s == 0 and has_acc:
                        acc[lo:hi, c : c + n] = start[lo:hi, c : c + n] + d
                    elif s == 0:
                        acc[lo:hi, c : c + n] = d
                    else:
                        acc[lo:hi, c : c + n] += d
            if is_last and s == len(plan) - 1:
                outs[0][...] = acc[:, :nq].astype(jnp.bfloat16)
                outs[1][...] = acc[:, nq : nq + nk].astype(jnp.bfloat16)
                outs[2][...] = acc[:, nq + nk :].astype(jnp.bfloat16)


def project(idx, first, rows, plan, xs, weights, after, start=None, is_last=False, grant=48):
    depth = xs[0].shape[1]
    nq, nk = weights[0].shape[1], weights[1].shape[1]
    whole = lambda a: pl.BlockSpec(a.shape, lambda i, s: (0, 0))
    weight = lambda n: pl.BlockSpec((depth, n), lambda i, s: (s[first + i], 0))
    result = lambda n: pl.BlockSpec((rows, n), lambda i, s: (0, 0))
    total = nq + 2 * nk
    if is_last:
        out_specs = [result(n) for n in (nq, nk, nk)]
        out_shape = [jax.ShapeDtypeStruct((rows, n), jnp.bfloat16) for n in (nq, nk, nk)]
        scratch = [pltpu.VMEM((rows, total), jnp.float32)]
    else:
        out_specs = result(total)
        out_shape = jax.ShapeDtypeStruct((rows, total), jnp.float32)
        scratch = []
    extra = [] if start is None else [start]
    steps = len(plan)
    return pl.pallas_call(
        functools.partial(project_kernel, plan, len(after), start is not None, is_last),
        grid_spec=pltpu.PrefetchScalarGridSpec(
            num_scalar_prefetch=1,
            grid=(steps,),
            in_specs=[whole(a) for a in xs]
            + [weight(nq), weight(nk), weight(nk)]
            + [whole(a) for a in extra]
            + [pl.BlockSpec(memory_space=pl.ANY) for _ in after],
            out_specs=out_specs,
            scratch_shapes=scratch,
        ),
        out_shape=out_shape,
        compiler_params=params(grant),
        cost_estimate=cost(2 * steps * rows * depth * total, 2 * steps * depth * (total + rows)),
    )(idx, *xs, *weights, *extra, *after)


FAR = DEPTH * SEG_LEN
HEADS = 2


def attend_kernel(slot_ref, q_ref, k_ref, v_ref, *refs):
    *tables, out_ref, keys, values = refs
    roll = pl.program_id(0)
    scale = math.log2(math.e) / math.sqrt(HD)
    slot = lax.broadcasted_iota(jnp.int32, (1, SEG_LEN), 1)
    masks = []
    for level in range(DEPTH):
        at = roll * DEPTH + level
        live = slot_ref[PARTS, at]
        row = slot
        if level % 2:
            row = (PARTS - 1 - slot // GRAN) * GRAN + slot % GRAN
        masks.append(jnp.where(row < live, 0.0, -jnp.inf))
        pieces = []
        for i in range(PARTS):
            to = slot_ref[i, at]
            piece = tables[0][i, jnp.minimum(to, SECOND - 1)]
            if len(tables) > 1:
                rest = tables[1][i, jnp.maximum(to - SECOND, 0)]
                piece = jnp.where(to < SECOND, piece, rest)
            pieces.append(piece)
        lo = level * SEG_LEN
        keys[lo : lo + SEG_LEN] = jnp.concatenate([p[:GRAN] for p in pieces], axis=0)
        values[lo : lo + SEG_LEN] = jnp.concatenate([p[GRAN:] for p in pieces], axis=0)
    mask = jnp.concatenate(masks, axis=1)
    row = lax.broadcasted_iota(jnp.int32, (ROLL, ROLL), 0)
    causal = jnp.where(row >= lax.broadcasted_iota(jnp.int32, (ROLL, ROLL), 1), 0.0, -jnp.inf)
    causal = jnp.concatenate([causal] * HEADS, axis=0)
    nt = (((1,), (1,)), ((), ()))
    ones = jnp.ones((FAR, HD), jnp.bfloat16)
    for g0 in range(0, GROUP, HEADS):
        heads = range(g0, g0 + HEADS)
        q = jnp.concatenate([q_ref[:, g * HD : (g + 1) * HD] for g in heads], axis=0)
        far = lax.dot_general(q, keys[...], nt, preferred_element_type=jnp.float32) + mask
        own = lax.dot_general(q, k_ref[...], nt, preferred_element_type=jnp.float32) + causal
        m = jnp.maximum(jnp.max(far, axis=1, keepdims=True), jnp.max(own, axis=1, keepdims=True))
        far = jnp.exp2((far - m) * scale).astype(jnp.bfloat16)
        own = jnp.exp2((own - m) * scale).astype(jnp.bfloat16)
        far_values = jnp.concatenate([values[...], ones], axis=1)
        own_values = jnp.concatenate([v_ref[...], ones[:ROLL]], axis=1)
        mix = jnp.dot(far, far_values, preferred_element_type=jnp.float32)
        mix += jnp.dot(own, own_values, preferred_element_type=jnp.float32)
        mix = (mix[:, :HD] / mix[:, HD:]).astype(jnp.bfloat16)
        for n, g in enumerate(heads):
            out_ref[:, g * HD : (g + 1) * HD] = mix[n * ROLL : (n + 1) * ROLL]


def attend(slots, q, k, v, tables):
    rolls = q.shape[0] // ROLL
    row = lambda n: pl.BlockSpec((ROLL, n), lambda i, *s: (i, 0))
    return pl.pallas_call(
        attend_kernel,
        grid_spec=pltpu.PrefetchScalarGridSpec(
            num_scalar_prefetch=1,
            grid=(rolls,),
            in_specs=[row(GROUP * HD), row(HD), row(HD)]
            + [pl.BlockSpec(t.shape, lambda i, *s: (0, 0, 0, 0)) for t in tables],
            out_specs=row(GROUP * HD),
            scratch_shapes=[
                pltpu.VMEM((FAR, HD), jnp.bfloat16),
                pltpu.VMEM((FAR, HD), jnp.bfloat16),
            ],
        ),
        out_shape=jax.ShapeDtypeStruct(q.shape, jnp.bfloat16),
        compiler_params=params(48),
        cost_estimate=cost(
            4 * q.size * (DEPTH * SEG_LEN + ROLL), 4 * (q.size + tables[0].size)
        ),
    )(slots, q, k, v, *tables)


def terms_kernel(count, added, skip, outs, idx_ref, a_ref, b_ref, *refs):
    w_own, w_sib, refs = refs[:count], refs[count : 2 * count], refs[2 * count :]
    more, results = refs[:added], refs[added + skip :]
    for k in range(count):
        acc = jnp.dot(a_ref[...], w_own[k][...], preferred_element_type=jnp.float32)
        acc += jnp.dot(b_ref[...], w_sib[k][...], preferred_element_type=jnp.float32)
        for n, ((which, lo, hi, dtype), out_ref) in enumerate(zip(outs, results)):
            if which == k:
                term = acc[lo:hi]
                if added:
                    term += more[n][...].astype(jnp.float32)
                out_ref[...] = term.astype(dtype)


def terms(idx, first, count, outs, added, after, own, sib, w_own, w_sib):
    rows, depth = own.shape
    width = w_own.shape[1] // (2 * RING)
    cut = 2
    tile = width // cut
    left = pl.BlockSpec((rows, depth), lambda j, s: (0, 0))
    weight = lambda k: pl.BlockSpec((depth, tile), lambda j, s: (0, s[8 + first + k] * cut + j))
    return pl.pallas_call(
        functools.partial(terms_kernel, count, len(added), len(after), outs),
        grid_spec=pltpu.PrefetchScalarGridSpec(
            num_scalar_prefetch=1,
            grid=(cut,),
            in_specs=[left, left]
            + [weight(k) for k in range(count)] * 2
            + [pl.BlockSpec((x.shape[0], tile), lambda j, s: (0, j)) for x in added]
            + [pl.BlockSpec(memory_space=pl.ANY) for _ in after],
            out_specs=[pl.BlockSpec((hi - lo, tile), lambda j, s: (0, j)) for _, lo, hi, _ in outs],
        ),
        out_shape=[jax.ShapeDtypeStruct((hi - lo, width), dtype) for _, lo, hi, dtype in outs],
        compiler_params=params(56),
        cost_estimate=cost(
            4 * count * rows * depth * width, 4 * count * depth * width + 4 * count * rows * width
        ),
    )(idx, own, sib, *([w_own] * count), *([w_sib] * count), *added, *after)


def add_terms(x, *received):
    for r in received:
        x = x + r.astype(jnp.float32)
    return x.astype(jnp.bfloat16)


def summed(idx, own, sib, w_own, w_sib):
    rows = own.shape[0]
    half = rows // 2
    f32, b16 = jnp.float32, jnp.bfloat16
    args = (own, sib, w_own, w_sib)
    far_outs = ((0, 0, half, b16), (0, half, rows, b16))
    far_top, far_bottom = terms(idx, 0, 1, far_outs, [], [], *args)
    via_up = send(far_top, UP)
    via_down = send(far_bottom, DOWN)
    near_outs = ((0, 0, half, f32), (0, half, rows, b16), (1, 0, half, b16), (1, half, rows, f32))
    next_top, next_bottom, prev_top, prev_bottom = terms(idx, 1, 2, near_outs, [], [far_top], *args)
    low_bottom = send(next_bottom, UP)
    up_top = send(prev_top, DOWN)
    mine_outs = ((0, 0, half, f32), (0, half, rows, f32))
    mine_top, mine_bottom = terms(idx, 3, 1, mine_outs, [up_top, low_bottom], [], *args)
    low_top = send(add_terms(next_top, via_up), UP)
    up_bottom = send(add_terms(prev_bottom, via_down), DOWN)
    out = [add_terms(mine_top, low_top), add_terms(mine_bottom, up_bottom)]
    return jnp.concatenate(out, axis=0)


def per_device(
    hidden, w_query, w_key, w_value, w_out, prefix_keys, prefix_values, seg_lengths, ancestors
):
    head = lax.axis_index("head")
    idx = lax.dynamic_index_in_dim(jnp.asarray(index_table()), head, 0, keepdims=False)
    chain = ancestors.reshape(-1)
    rows = hidden.shape[0]
    half = rows // 2
    weights = (w_query, w_key, w_value)
    whole = ((0, rows),)
    split = ((0, half), (half, rows))

    low = send(hidden, UP)
    up = send(hidden, DOWN)
    sib = send(hidden, SIBLING)

    w_sib = send(w_out, SIBLING)

    for_pack, for_pick, for_attend, most = number_pieces(chain, seg_lengths)
    table = exchange(pack(0, FIRST, for_pack, prefix_keys, prefix_values))

    low_half, up_half = low[:half], up[half:]

    def rest():
        return exchange(pack(FIRST, PARTS, for_pack, prefix_keys, prefix_values))

    def pick_all(lo, hi, tables):
        return pick(lo, hi, for_pick, tables, [low_half, up_half, idx])

    picked = lax.cond(
        most[0] > FIRST,
        lambda: pick_all(0, SECOND, [table, rest()]),
        lambda: pick_all(0, SECOND, [table]),
    )
    far = exchange(picked)

    near_blocks = [hidden, sib, low, send(low, SIBLING), up, send(up, SIBLING)]
    acc = project(idx, 0, rows, (whole,) * 6, near_blocks, weights, [])

    far_top, far_bottom = ordered([send(low_half, UP), send(up_half, DOWN)], acc)
    far_blocks = [far_top, far_bottom, send(far_top, SIBLING), send(far_bottom, SIBLING)]
    q, k, v = project(idx, 6, rows, (split,) * 2, far_blocks, weights, [], acc, True, 60)

    def attend_rest():
        far_rest = exchange(pick_all(SECOND, PARTS, [table, rest()]))
        return attend(for_attend, q, k, v, [far, far_rest])

    def attend_all():
        return attend(for_attend, q, k, v, [far])

    own = lax.cond(most[1] > SECOND, attend_rest, attend_all)
    return summed(idx, own, send(own, SIBLING), w_out, w_sib)


def solution(mesh):
    in_specs = (
        P("seq", "head"),
        P(None, "head"),
        P(None, "head"),
        P(None, "head"),
        P("head", None),
        P("seq", "head"),
        P("seq", "head"),
        P(),
        P(),
    )
    out_specs = P("seq", "head")
    return jax.shard_map(
        per_device, mesh=mesh, in_specs=in_specs, out_specs=out_specs, check_vma=False
    )
```

```python
import functools
import math

import jax
import jax.numpy as jnp
import numpy as np
from jax import lax
from jax.experimental import pallas as pl
from jax.experimental.pallas import tpu as pltpu
from jax.sharding import PartitionSpec as P

QH = 32
KVH = 8
HD = 128
ROLL = 128
SEG_LEN = 256
DEPTH = 4
GROUP = QH // KVH
GRAN = 16

RING = 4


def y_shift(step):
    return [(y * 2 + c, ((y + step) % RING) * 2 + c) for y in range(RING) for c in range(2)]


SIBLING = [(h, h ^ 1) for h in range(2 * RING)]
UP = y_shift(1)
DOWN = y_shift(-1)


def send(x, pairs):
    return lax.ppermute(x, "head", pairs)


def params(mib):
    return pltpu.CompilerParams(vmem_limit_bytes=mib * 1024 * 1024)


def cost(flops, nbytes):
    return pl.CostEstimate(flops=int(flops), bytes_accessed=int(nbytes), transcendentals=0)


def index_table():
    rows = []
    for h in range(2 * RING):
        y, c = divmod(h, 2)
        row = []
        for other in (y, (y - 1) % RING, (y + 1) % RING, (y + 2) % RING):
            row += [2 * other + c, 2 * other + 1 - c]
        order = [(y + 2) % RING, (y + 1) % RING, (y - 1) % RING, y]
        row += [2 * t + c for t in order]
        rows.append(row)
    return np.asarray(rows, np.int32)


def ordered_kernel(*refs):
    pass


def ordered(xs, after):
    anywhere = pl.BlockSpec(memory_space=pl.ANY)
    return pl.pallas_call(
        ordered_kernel,
        in_specs=[anywhere] * (len(xs) + 1),
        out_specs=[anywhere] * len(xs),
        out_shape=[jax.ShapeDtypeStruct(x.shape, x.dtype) for x in xs],
        input_output_aliases={n: n for n in range(len(xs))},
        cost_estimate=cost(0, 0),
    )(*xs, after)


FIRST = 9
SECOND = 13
PARTS = SEG_LEN // GRAN
STEPS = 4
BATCH = 8


def table_kernel(chain_ref, len_ref, pack_ref, pick_ref, attend_ref, most_ref):
    f32, b16 = jnp.float32, jnp.bfloat16
    me = lax.axis_index("seq")
    chain = chain_ref[...]
    count = chain.shape[1]
    segs = len_ref.shape[1]
    iota = lambda shape, axis: lax.broadcasted_iota(jnp.int32, shape, axis)
    exact = lambda x, y: jnp.dot(x.astype(b16), y, preferred_element_type=f32)
    wants = jnp.where(iota((segs, count), 0) == chain, 1.0, 0.0).astype(b16)
    uses = lax.dot_general(
        jnp.ones((8, count), b16), wants, (((1,), (1,)), ((), ())), preferred_element_type=f32
    )[:1]
    lengths = len_ref[...].astype(f32)
    pieces = jnp.floor((lengths + (GRAN - 1)) * (1.0 / GRAN))
    live = exact(jnp.broadcast_to(lengths, (8, segs)), wants)
    row, col = iota((segs, segs), 0), iota((segs, segs), 1)
    earlier = jnp.where((row // PARTS == col // PARTS) & (row < col), 1.0, 0.0).astype(b16)
    mine = iota((segs, 128), 1)
    mine = jnp.where((iota((segs, 128), 0) == me * PARTS + mine) & (mine < PARTS), 1.0, 0.0)
    mine = mine.astype(b16)

    def number(level, held):
        device = iota((PARTS, segs), 0).astype(f32)
        piece = jnp.where(level % 2 == 1, (PARTS - 1) - device, device)
        counts = jnp.where(piece < held, 1.0, 0.0)
        before = exact(counts, earlier)
        return before, jnp.max(before + counts).astype(jnp.int32)

    def kept(x):
        return jnp.sum(jnp.where(iota(x.shape, 0) == me, x, 0.0), axis=0, keepdims=True)

    first, most_first = number(iota((1, segs), 1), jnp.where(uses > 0.0, pieces, 0.0))
    slot_pieces = jnp.floor((live[:1] + (GRAN - 1)) * (1.0 / GRAN))
    second, most_second = number(jnp.maximum(chain, 0), slot_pieces)
    source = jnp.maximum(chain, 0) // PARTS
    place = source * PARTS + kept(exact(first, wants)).astype(jnp.int32)
    to = kept(second).astype(jnp.int32)
    most = [jnp.full((1, segs), m, jnp.int32) for m in (most_first, most_second)]
    at = place - source * PARTS
    from_row = source * FIRST + jnp.minimum(at, FIRST - 1)
    to_row = (iota((1, segs), 1) // PARTS) % (PARTS // STEPS) * SECOND + to
    pick_ref[...] = jnp.concatenate([place, to] + most + [from_row, to_row] * 2, axis=0)
    pack_ref[:PARTS] = exact(first, mine).astype(jnp.int32)
    pack_ref[PARTS:] = jnp.full((8, 128), most_first, jnp.int32)
    attend_ref[:PARTS] = exact(second, mine).astype(jnp.int32)
    attend_ref[PARTS:] = exact(live, mine).astype(jnp.int32)
    most_ref[0] = most_first
    most_ref[1] = most_second


def number_pieces(chain, lengths):
    vmem = pl.BlockSpec(memory_space=pltpu.VMEM)
    own = jax.ShapeDtypeStruct((PARTS + 8, 128), jnp.int32)
    return pl.pallas_call(
        table_kernel,
        out_specs=[vmem, vmem, vmem, pl.BlockSpec(memory_space=pltpu.SMEM)],
        out_shape=[
            own,
            jax.ShapeDtypeStruct((8, chain.size), jnp.int32),
            own,
            jax.ShapeDtypeStruct((2,), jnp.int32),
        ],
        compiler_params=params(32),
        cost_estimate=cost(0, 0),
    )(chain.reshape(1, -1), lengths.reshape(1, -1))


def pack_kernel(lo, hi, first_ref, k0_ref, k1_ref, v0_ref, v1_ref, out_ref):
    pairs, _, step = k0_ref.shape[:3]
    block = pl.program_id(0) * step

    def piece_of(j, i):
        odd = j % 2
        piece = step - 1 - i if odd else i
        return (k0_ref, k1_ref)[odd][j // 2, 0, piece], (v0_ref, v1_ref)[odd][j // 2, 0, piece]

    def put(i, at, pair):
        out_ref[i, at, :GRAN] = pair[0]
        out_ref[i, at, GRAN:] = pair[1]

    def guarded(i, carry):
        for j in range(2 * pairs):
            at = first_ref[block + i, j]
            pl.when((at >= lo) & (at < hi))(lambda: put(i, at - lo, piece_of(j, i)))
        return carry

    def plain():
        for i in range(step):
            for j0 in range(0, 2 * pairs, BATCH):
                batch = range(j0, j0 + BATCH)
                at = [first_ref[block + i, j] for j in batch]
                for a, pair in zip(at, [piece_of(j, i) for j in batch]):
                    put(i, a, pair)

    most = first_ref[PARTS, 0]
    if lo == 0:
        pl.when(most < hi)(plain)
        pl.when(most >= hi)(lambda: lax.fori_loop(0, step, guarded, None))
    else:
        lax.fori_loop(0, step, guarded, None)


def pack(lo, hi, first, keys, values):
    segs = keys.shape[0] // SEG_LEN
    steps = 4
    step = PARTS // steps
    view = (segs // 2, 2, PARTS, GRAN, HD)
    block = (segs // 2, 1, step, GRAN, HD)
    even = pl.BlockSpec(block, lambda i, *s: (0, 0, i, 0, 0))
    odd = pl.BlockSpec(block, lambda i, *s: (0, 1, steps - 1 - i, 0, 0))
    shape = (PARTS, hi - lo, 2 * GRAN, HD)
    keys, values = keys.reshape(view), values.reshape(view)
    return pl.pallas_call(
        functools.partial(pack_kernel, lo, hi),
        grid_spec=pltpu.PrefetchScalarGridSpec(
            num_scalar_prefetch=1,
            grid=(steps,),
            in_specs=[even, odd, even, odd],
            out_specs=pl.BlockSpec((step,) + shape[1:], lambda i, *s: (i, 0, 0, 0)),
        ),
        out_shape=jax.ShapeDtypeStruct(shape, jnp.bfloat16),
        compiler_params=params(60),
        cost_estimate=cost(0, 4 * keys.size * 2),
    )(first, keys, keys, values, values)


def pick_kernel(lo, hi, split, slot_ref, *refs):
    table_ref, out_ref = refs[0], refs[-1]
    devices = out_ref.shape[0]
    slots = slot_ref.shape[1] // PARTS
    base = pl.program_id(0) * devices

    def piece_of(place):
        source, at = place // PARTS, place % PARTS
        piece = table_ref[source, jnp.minimum(at, FIRST - 1)]
        if split:
            rest = refs[1][source, jnp.maximum(at - FIRST, 0)]
            piece = jnp.where(at < FIRST, piece, rest)
        return piece

    def put(d, to, piece):
        out_ref[d, to] = piece

    def guarded(d, carry):
        for n in range(slots):
            slot = (base + d) * slots + n
            to = slot_ref[1, slot]
            pl.when((to >= lo) & (to < hi))(lambda: put(d, to - lo, piece_of(slot_ref[0, slot])))
        return carry

    def plain():
        flat = table_ref.reshape(PARTS * FIRST, 2 * GRAN, HD)
        out = out_ref.reshape(devices * (hi - lo), 2 * GRAN, HD)
        for n0 in range(0, devices * slots, BATCH):
            batch = [base * slots + n for n in range(n0, n0 + BATCH)]
            pieces = [flat[slot_ref[4, slot]] for slot in batch]
            for slot, piece in zip(batch, pieces):
                out[slot_ref[5, slot]] = piece

    most = slot_ref[3, 0]
    if lo == 0 and not split:
        pl.when(most < hi)(plain)
        pl.when(most >= hi)(lambda: lax.fori_loop(0, devices, guarded, None))
    else:
        lax.fori_loop(0, devices, guarded, None)


def pick(lo, hi, slots, tables, after):
    steps = STEPS
    shape = (PARTS, hi - lo, 2 * GRAN, HD)
    return pl.pallas_call(
        functools.partial(pick_kernel, lo, hi, len(tables) > 1),
        grid_spec=pltpu.PrefetchScalarGridSpec(
            num_scalar_prefetch=1,
            grid=(steps,),
            in_specs=[pl.BlockSpec(t.shape, lambda i, *s: (0, 0, 0, 0)) for t in tables]
            + [pl.BlockSpec(memory_space=pl.ANY) for _ in after],
            out_specs=pl.BlockSpec((PARTS // steps,) + shape[1:], lambda i, *s: (i, 0, 0, 0)),
        ),
        out_shape=jax.ShapeDtypeStruct(shape, jnp.bfloat16),
        compiler_params=params(60),
        cost_estimate=cost(0, 4 * tables[0].size),
    )(slots, *tables, *after)


def exchange(x):
    return lax.all_to_all(x, "seq", 0, 0, tiled=True)


def project_kernel(plan, skip, has_acc, is_last, idx_ref, *refs):
    count = sum(len(pieces) for pieces in plan)
    xs = refs[:count]
    wq, wk, wv = refs[count : count + 3]
    rest = refs[count + 3 :]
    start = rest[0] if has_acc else None
    outs = rest[skip + has_acc :]
    acc = outs[-1]
    step = pl.program_id(0)
    nq = wq.shape[1]
    nk = wk.shape[1]
    at = 0
    for s, pieces in enumerate(plan):
        mine = xs[at : at + len(pieces)]
        at += len(pieces)

        @pl.when(step == s)
        def _():
            for (lo, hi), x in zip(pieces, mine):
                for w, c, n in ((wq, 0, nq), (wk, nq, nk), (wv, nq + nk, nk)):
                    d = jnp.dot(x[...], w[...], preferred_element_type=jnp.float32)
                    if s == 0 and has_acc:
                        acc[lo:hi, c : c + n] = start[lo:hi, c : c + n] + d
                    elif s == 0:
                        acc[lo:hi, c : c + n] = d
                    else:
                        acc[lo:hi, c : c + n] += d
            if is_last and s == len(plan) - 1:
                outs[0][...] = acc[:, :nq].astype(jnp.bfloat16)
                outs[1][...] = acc[:, nq : nq + nk].astype(jnp.bfloat16)
                outs[2][...] = acc[:, nq + nk :].astype(jnp.bfloat16)


def project(idx, first, rows, plan, xs, weights, after, start=None, is_last=False, grant=48):
    depth = xs[0].shape[1]
    nq, nk = weights[0].shape[1], weights[1].shape[1]
    whole = lambda a: pl.BlockSpec(a.shape, lambda i, s: (0, 0))
    weight = lambda n: pl.BlockSpec((depth, n), lambda i, s: (s[first + i], 0))
    result = lambda n: pl.BlockSpec((rows, n), lambda i, s: (0, 0))
    total = nq + 2 * nk
    if is_last:
        out_specs = [result(n) for n in (nq, nk, nk)]
        out_shape = [jax.ShapeDtypeStruct((rows, n), jnp.bfloat16) for n in (nq, nk, nk)]
        scratch = [pltpu.VMEM((rows, total), jnp.float32)]
    else:
        out_specs = result(total)
        out_shape = jax.ShapeDtypeStruct((rows, total), jnp.float32)
        scratch = []
    extra = [] if start is None else [start]
    steps = len(plan)
    return pl.pallas_call(
        functools.partial(project_kernel, plan, len(after), start is not None, is_last),
        grid_spec=pltpu.PrefetchScalarGridSpec(
            num_scalar_prefetch=1,
            grid=(steps,),
            in_specs=[whole(a) for a in xs]
            + [weight(nq), weight(nk), weight(nk)]
            + [whole(a) for a in extra]
            + [pl.BlockSpec(memory_space=pl.ANY) for _ in after],
            out_specs=out_specs,
            scratch_shapes=scratch,
        ),
        out_shape=out_shape,
        compiler_params=params(grant),
        cost_estimate=cost(2 * steps * rows * depth * total, 2 * steps * depth * (total + rows)),
    )(idx, *xs, *weights, *extra, *after)


FAR = DEPTH * SEG_LEN
HEADS = 2


def attend_kernel(slot_ref, q_ref, k_ref, v_ref, *refs):
    *tables, out_ref, keys, values = refs
    scale = math.log2(math.e) / math.sqrt(HD)
    slot = lax.broadcasted_iota(jnp.int32, (1, SEG_LEN), 1)

    def rollout(roll, carry):
        tokens = pl.ds(pl.multiple_of(roll * ROLL, ROLL), ROLL)
        masks = []
        for level in range(DEPTH):
            at = roll * DEPTH + level
            live = slot_ref[PARTS, at]
            row = slot
            if level % 2:
                row = (PARTS - 1 - slot // GRAN) * GRAN + slot % GRAN
            masks.append(jnp.where(row < live, 0.0, -jnp.inf))
            pieces = []
            for i in range(PARTS):
                to = slot_ref[i, at]
                piece = tables[0][i, jnp.minimum(to, SECOND - 1)]
                if len(tables) > 1:
                    rest = tables[1][i, jnp.maximum(to - SECOND, 0)]
                    piece = jnp.where(to < SECOND, piece, rest)
                pieces.append(piece)
            lo = level * SEG_LEN
            keys[lo : lo + SEG_LEN] = jnp.concatenate([p[:GRAN] for p in pieces], axis=0)
            values[lo : lo + SEG_LEN] = jnp.concatenate([p[GRAN:] for p in pieces], axis=0)
        mask = jnp.concatenate(masks, axis=1)
        row = lax.broadcasted_iota(jnp.int32, (ROLL, ROLL), 0)
        causal = jnp.where(row >= lax.broadcasted_iota(jnp.int32, (ROLL, ROLL), 1), 0.0, -jnp.inf)
        causal = jnp.concatenate([causal] * HEADS, axis=0)
        nt = (((1,), (1,)), ((), ()))
        ones = jnp.ones((FAR, HD), jnp.bfloat16)
        for g0 in range(0, GROUP, HEADS):
            heads = range(g0, g0 + HEADS)
            q = jnp.concatenate([q_ref[tokens, g * HD : (g + 1) * HD] for g in heads], axis=0)
            far = lax.dot_general(q, keys[...], nt, preferred_element_type=jnp.float32) + mask
            own = lax.dot_general(q, k_ref[tokens], nt, preferred_element_type=jnp.float32) + causal
            m = jnp.maximum(jnp.max(far, axis=1, keepdims=True), jnp.max(own, axis=1, keepdims=True))
            far = jnp.exp2((far - m) * scale).astype(jnp.bfloat16)
            own = jnp.exp2((own - m) * scale).astype(jnp.bfloat16)
            far_values = jnp.concatenate([values[...], ones], axis=1)
            own_values = jnp.concatenate([v_ref[tokens], ones[:ROLL]], axis=1)
            mix = jnp.dot(far, far_values, preferred_element_type=jnp.float32)
            mix += jnp.dot(own, own_values, preferred_element_type=jnp.float32)
            mix = (mix[:, :HD] / mix[:, HD:]).astype(jnp.bfloat16)
            for n, g in enumerate(heads):
                out_ref[tokens, g * HD : (g + 1) * HD] = mix[n * ROLL : (n + 1) * ROLL]
        return carry

    lax.fori_loop(0, q_ref.shape[0] // ROLL, rollout, None)


def attend(slots, q, k, v, tables):
    vmem = pl.BlockSpec(memory_space=pltpu.VMEM)
    return pl.pallas_call(
        attend_kernel,
        in_specs=[pl.BlockSpec(memory_space=pltpu.SMEM)] + [vmem] * (3 + len(tables)),
        out_specs=vmem,
        scratch_shapes=[
            pltpu.VMEM((FAR, HD), jnp.bfloat16),
            pltpu.VMEM((FAR, HD), jnp.bfloat16),
        ],
        out_shape=jax.ShapeDtypeStruct(q.shape, jnp.bfloat16),
        compiler_params=params(48),
        cost_estimate=cost(
            4 * q.size * (DEPTH * SEG_LEN + ROLL), 4 * (q.size + tables[0].size)
        ),
    )(slots, q, k, v, *tables)


def terms_kernel(count, added, skip, outs, idx_ref, a_ref, b_ref, *refs):
    w_own, w_sib, refs = refs[:count], refs[count : 2 * count], refs[2 * count :]
    more, results = refs[:added], refs[added + skip :]
    for k in range(count):
        acc = jnp.dot(a_ref[...], w_own[k][...], preferred_element_type=jnp.float32)
        acc += jnp.dot(b_ref[...], w_sib[k][...], preferred_element_type=jnp.float32)
        for n, ((which, lo, hi, dtype), out_ref) in enumerate(zip(outs, results)):
            if which == k:
                term = acc[lo:hi]
                if added:
                    term += more[n][...].astype(jnp.float32)
                out_ref[...] = term.astype(dtype)


def terms(idx, first, count, outs, added, after, own, sib, w_own, w_sib):
    rows, depth = own.shape
    width = w_own.shape[1] // (2 * RING)
    cut = 2
    tile = width // cut
    left = pl.BlockSpec((rows, depth), lambda j, s: (0, 0))
    weight = lambda k: pl.BlockSpec((depth, tile), lambda j, s: (0, s[8 + first + k] * cut + j))
    return pl.pallas_call(
        functools.partial(terms_kernel, count, len(added), len(after), outs),
        grid_spec=pltpu.PrefetchScalarGridSpec(
            num_scalar_prefetch=1,
            grid=(cut,),
            in_specs=[left, left]
            + [weight(k) for k in range(count)] * 2
            + [pl.BlockSpec((x.shape[0], tile), lambda j, s: (0, j)) for x in added]
            + [pl.BlockSpec(memory_space=pl.ANY) for _ in after],
            out_specs=[pl.BlockSpec((hi - lo, tile), lambda j, s: (0, j)) for _, lo, hi, _ in outs],
        ),
        out_shape=[jax.ShapeDtypeStruct((hi - lo, width), dtype) for _, lo, hi, dtype in outs],
        compiler_params=params(53),
        cost_estimate=cost(
            4 * count * rows * depth * width, 4 * count * depth * width + 4 * count * rows * width
        ),
    )(idx, own, sib, *([w_own] * count), *([w_sib] * count), *added, *after)


def own_term_kernel(low_rows, own_ref, sib_ref, wa_ref, wb_ref, up_ref, low_ref, top_ref, bottom_ref, w_ref, sems):
    width = w_ref.shape[-1] // 2
    head = lax.axis_index("head")
    loads = []
    for part in range(2):
        at = pl.ds(pl.multiple_of(head * (2 * width) + part * width, width), width)
        to = pl.ds(part * width, width)
        for n, ref in enumerate((wa_ref, wb_ref)):
            loads.append(pltpu.make_async_copy(ref.at[:, at], w_ref.at[n, :, to], sems.at[part, n]))
            loads[-1].start()
    for part in range(2):
        for load in loads[2 * part : 2 * part + 2]:
            load.wait()
        to = slice(part * width, (part + 1) * width)
        acc = jnp.dot(own_ref[...], w_ref[0, :, to], preferred_element_type=jnp.float32)
        acc += jnp.dot(sib_ref[...], w_ref[1, :, to], preferred_element_type=jnp.float32)
        top_ref[:, to] = acc[:low_rows] + up_ref[:, to].astype(jnp.float32)
        bottom_ref[:, to] = acc[low_rows:] + low_ref[:, to].astype(jnp.float32)


def own_term(own, sib, w_own, w_sib, up_top, low_bottom):
    rows, depth = own.shape
    half, width = up_top.shape
    vmem = pl.BlockSpec(memory_space=pltpu.VMEM)
    hbm = pl.BlockSpec(memory_space=pl.ANY)
    return pl.pallas_call(
        functools.partial(own_term_kernel, half),
        in_specs=[vmem, vmem, hbm, hbm, vmem, vmem],
        out_specs=[vmem, vmem],
        out_shape=[jax.ShapeDtypeStruct((half, width), jnp.float32)] * 2,
        scratch_shapes=[
            pltpu.VMEM((2, depth, width), jnp.bfloat16),
            pltpu.SemaphoreType.DMA((2, 2)),
        ],
        compiler_params=params(16),
        cost_estimate=cost(4 * rows * depth * width, 4 * depth * width + 4 * rows * width),
    )(own, sib, w_own, w_sib, up_top, low_bottom)


def add_terms(x, *received):
    for r in received:
        x = x + r.astype(jnp.float32)
    return x.astype(jnp.bfloat16)


def finish_kernel(mine_top, low_top, mine_bottom, up_bottom, out_ref, rows_ref, sems):
    half = mine_top.shape[0]
    tile = half // 2
    stores = []
    for n, (mine, received) in enumerate(((mine_top, low_top), (mine_bottom, up_bottom))):
        for part in range(2):
            rows = slice(part * tile, (part + 1) * tile)
            to = pl.ds(n * half + part * tile, tile)
            total = mine[rows] + received[rows].astype(jnp.float32)
            rows_ref[to] = total.astype(jnp.bfloat16)
            store = pltpu.make_async_copy(rows_ref.at[to], out_ref.at[to], sems.at[n, part])
            store.start()
            stores.append(store)
    for store in stores:
        store.wait()


def finish(mine_top, low_top, mine_bottom, up_bottom):
    vmem = pl.BlockSpec(memory_space=pltpu.VMEM)
    half, width = mine_top.shape
    shape = (2 * half, width)
    return pl.pallas_call(
        finish_kernel,
        in_specs=[vmem] * 4,
        out_specs=pl.BlockSpec(memory_space=pl.ANY),
        out_shape=jax.ShapeDtypeStruct(shape, jnp.bfloat16),
        scratch_shapes=[pltpu.VMEM(shape, jnp.bfloat16), pltpu.SemaphoreType.DMA((2, 2))],
        compiler_params=params(16),
        cost_estimate=cost(0, 16 * mine_top.size),
    )(mine_top, low_top, mine_bottom, up_bottom)


def summed(idx, own, sib, w_own, w_sib):
    rows = own.shape[0]
    half = rows // 2
    f32, b16 = jnp.float32, jnp.bfloat16
    args = (own, sib, w_own, w_sib)
    far_outs = ((0, 0, half, b16), (0, half, rows, b16))
    far_top, far_bottom = terms(idx, 0, 1, far_outs, [], [], *args)
    via_up = send(far_top, UP)
    via_down = send(far_bottom, DOWN)
    near_outs = ((0, 0, half, f32), (0, half, rows, b16), (1, 0, half, b16), (1, half, rows, f32))
    next_top, next_bottom, prev_top, prev_bottom = terms(idx, 1, 2, near_outs, [], [far_top], *args)
    low_bottom = send(next_bottom, UP)
    up_top = send(prev_top, DOWN)
    mine_top, mine_bottom = own_term(*args, up_top, low_bottom)
    low_top = send(add_terms(next_top, via_up), UP)
    up_bottom = send(add_terms(prev_bottom, via_down), DOWN)
    return finish(mine_top, low_top, mine_bottom, up_bottom)


def per_device(
    hidden, w_query, w_key, w_value, w_out, prefix_keys, prefix_values, seg_lengths, ancestors
):
    head = lax.axis_index("head")
    idx = lax.dynamic_index_in_dim(jnp.asarray(index_table()), head, 0, keepdims=False)
    chain = ancestors.reshape(-1)
    rows = hidden.shape[0]
    half = rows // 2
    weights = (w_query, w_key, w_value)
    whole = ((0, rows),)
    split = ((0, half), (half, rows))

    low = send(hidden, UP)
    up = send(hidden, DOWN)
    sib = send(hidden, SIBLING)

    w_sib = send(w_out, SIBLING)

    for_pack, for_pick, for_attend, most = number_pieces(chain, seg_lengths)
    table = exchange(pack(0, FIRST, for_pack, prefix_keys, prefix_values))

    low_half, up_half = low[:half], up[half:]

    def rest():
        return exchange(pack(FIRST, PARTS, for_pack, prefix_keys, prefix_values))

    def pick_all(lo, hi, tables):
        return pick(lo, hi, for_pick, tables, [low_half, up_half, idx])

    picked = lax.cond(
        most[0] > FIRST,
        lambda: pick_all(0, SECOND, [table, rest()]),
        lambda: pick_all(0, SECOND, [table]),
    )
    far = exchange(picked)

    near_blocks = [hidden, sib, low, send(low, SIBLING), up, send(up, SIBLING)]
    acc = project(idx, 0, rows, (whole,) * 6, near_blocks, weights, [])

    far_top, far_bottom = ordered([send(low_half, UP), send(up_half, DOWN)], acc)
    far_blocks = [far_top, far_bottom, send(far_top, SIBLING), send(far_bottom, SIBLING)]
    q, k, v = project(idx, 6, rows, (split,) * 2, far_blocks, weights, [], acc, True, 60)

    def attend_rest():
        far_rest = exchange(pick_all(SECOND, PARTS, [table, rest()]))
        return attend(for_attend, q, k, v, [far, far_rest])

    def attend_all():
        return attend(for_attend, q, k, v, [far])

    own = lax.cond(most[1] > SECOND, attend_rest, attend_all)
    return summed(idx, own, send(own, SIBLING), w_out, w_sib)


def solution(mesh):
    in_specs = (
        P("seq", "head"),
        P(None, "head"),
        P(None, "head"),
        P(None, "head"),
        P("head", None),
        P("seq", "head"),
        P("seq", "head"),
        P(),
        P(),
    )
    out_specs = P("seq", "head")
    return jax.shard_map(
        per_device, mesh=mesh, in_specs=in_specs, out_specs=out_specs, check_vma=False
    )
```

```python
import functools
import math

import jax
import jax.numpy as jnp
import numpy as np
from jax import lax
from jax.experimental import pallas as pl
from jax.experimental.pallas import tpu as pltpu
from jax.sharding import PartitionSpec as P

QH = 32
KVH = 8
HD = 128
ROLL = 128
SEG_LEN = 256
DEPTH = 4
GROUP = QH // KVH
GRAN = 16

RING = 4


def y_shift(step):
    return [(y * 2 + c, ((y + step) % RING) * 2 + c) for y in range(RING) for c in range(2)]


SIBLING = [(h, h ^ 1) for h in range(2 * RING)]
UP = y_shift(1)
DOWN = y_shift(-1)


def send(x, pairs):
    return lax.ppermute(x, "head", pairs)


def params(mib):
    return pltpu.CompilerParams(vmem_limit_bytes=mib * 1024 * 1024)


def cost(flops, nbytes):
    return pl.CostEstimate(flops=int(flops), bytes_accessed=int(nbytes), transcendentals=0)


def index_table():
    rows = []
    for h in range(2 * RING):
        y, c = divmod(h, 2)
        row = []
        for other in (y, (y - 1) % RING, (y + 1) % RING, (y + 2) % RING):
            row += [2 * other + c, 2 * other + 1 - c]
        order = [(y + 2) % RING, (y + 1) % RING, (y - 1) % RING, y]
        row += [2 * t + c for t in order]
        rows.append(row)
    return np.asarray(rows, np.int32)


def ordered_kernel(*refs):
    pass


def ordered(xs, after):
    anywhere = pl.BlockSpec(memory_space=pl.ANY)
    return pl.pallas_call(
        ordered_kernel,
        in_specs=[anywhere] * (len(xs) + 1),
        out_specs=[anywhere] * len(xs),
        out_shape=[jax.ShapeDtypeStruct(x.shape, x.dtype) for x in xs],
        input_output_aliases={n: n for n in range(len(xs))},
        cost_estimate=cost(0, 0),
    )(*xs, after)


FIRST = 9
SECOND = 13
PARTS = SEG_LEN // GRAN
STEPS = 4
BATCH = 8


def table_kernel(chain_ref, len_ref, pack_ref, pick_ref, attend_ref, most_ref):
    f32, b16 = jnp.float32, jnp.bfloat16
    me = lax.axis_index("seq")
    chain = chain_ref[...]
    count = chain.shape[1]
    segs = len_ref.shape[1]
    iota = lambda shape, axis: lax.broadcasted_iota(jnp.int32, shape, axis)
    exact = lambda x, y: jnp.dot(x.astype(b16), y, preferred_element_type=f32)
    wants = jnp.where(iota((segs, count), 0) == chain, 1.0, 0.0).astype(b16)
    uses = lax.dot_general(
        jnp.ones((8, count), b16), wants, (((1,), (1,)), ((), ())), preferred_element_type=f32
    )[:1]
    lengths = len_ref[...].astype(f32)
    pieces = jnp.floor((lengths + (GRAN - 1)) * (1.0 / GRAN))
    live = exact(jnp.broadcast_to(lengths, (8, segs)), wants)
    row, col = iota((segs, segs), 0), iota((segs, segs), 1)
    earlier = jnp.where((row // PARTS == col // PARTS) & (row < col), 1.0, 0.0).astype(b16)
    mine = iota((segs, 128), 1)
    mine = jnp.where((iota((segs, 128), 0) == me * PARTS + mine) & (mine < PARTS), 1.0, 0.0)
    mine = mine.astype(b16)

    def number(level, held):
        device = iota((PARTS, segs), 0).astype(f32)
        piece = jnp.where(level % 2 == 1, (PARTS - 1) - device, device)
        counts = jnp.where(piece < held, 1.0, 0.0)
        before = exact(counts, earlier)
        return before, jnp.max(before + counts).astype(jnp.int32)

    def kept(x):
        return jnp.sum(jnp.where(iota(x.shape, 0) == me, x, 0.0), axis=0, keepdims=True)

    first, most_first = number(iota((1, segs), 1), jnp.where(uses > 0.0, pieces, 0.0))
    slot_pieces = jnp.floor((live[:1] + (GRAN - 1)) * (1.0 / GRAN))
    second, most_second = number(jnp.maximum(chain, 0), slot_pieces)
    source = jnp.maximum(chain, 0) // PARTS
    place = source * PARTS + kept(exact(first, wants)).astype(jnp.int32)
    to = kept(second).astype(jnp.int32)
    most = [jnp.full((1, segs), m, jnp.int32) for m in (most_first, most_second)]
    at = place - source * PARTS
    from_row = source * FIRST + jnp.minimum(at, FIRST - 1)
    to_row = (iota((1, segs), 1) // PARTS) % (PARTS // STEPS) * SECOND + to
    pick_ref[...] = jnp.concatenate([place, to] + most + [from_row, to_row] * 2, axis=0)
    pack_ref[:PARTS] = exact(first, mine).astype(jnp.int32)
    pack_ref[PARTS:] = jnp.full((8, 128), most_first, jnp.int32)
    attend_ref[:PARTS] = exact(second, mine).astype(jnp.int32)
    attend_ref[PARTS:] = exact(live, mine).astype(jnp.int32)
    most_ref[0] = most_first
    most_ref[1] = most_second


def number_pieces(chain, lengths):
    vmem = pl.BlockSpec(memory_space=pltpu.VMEM)
    own = jax.ShapeDtypeStruct((PARTS + 8, 128), jnp.int32)
    return pl.pallas_call(
        table_kernel,
        out_specs=[vmem, vmem, vmem, pl.BlockSpec(memory_space=pltpu.SMEM)],
        out_shape=[
            own,
            jax.ShapeDtypeStruct((8, chain.size), jnp.int32),
            own,
            jax.ShapeDtypeStruct((2,), jnp.int32),
        ],
        compiler_params=params(32),
        cost_estimate=cost(0, 0),
    )(chain.reshape(1, -1), lengths.reshape(1, -1))


def pack_kernel(lo, hi, first_ref, k0_ref, k1_ref, v0_ref, v1_ref, out_ref):
    pairs, _, step = k0_ref.shape[:3]
    block = pl.program_id(0) * step

    def piece_of(j, i):
        odd = j % 2
        piece = step - 1 - i if odd else i
        return (k0_ref, k1_ref)[odd][j // 2, 0, piece], (v0_ref, v1_ref)[odd][j // 2, 0, piece]

    def put(i, at, pair):
        out_ref[i, at, :GRAN] = pair[0]
        out_ref[i, at, GRAN:] = pair[1]

    def guarded(i, carry):
        for j in range(2 * pairs):
            at = first_ref[block + i, j]
            pl.when((at >= lo) & (at < hi))(lambda: put(i, at - lo, piece_of(j, i)))
        return carry

    def plain():
        for i in range(step):
            for j0 in range(0, 2 * pairs, BATCH):
                batch = range(j0, j0 + BATCH)
                at = [first_ref[block + i, j] for j in batch]
                for a, pair in zip(at, [piece_of(j, i) for j in batch]):
                    put(i, a, pair)

    most = first_ref[PARTS, 0]
    if lo == 0:
        pl.when(most < hi)(plain)
        pl.when(most >= hi)(lambda: lax.fori_loop(0, step, guarded, None))
    else:
        lax.fori_loop(0, step, guarded, None)


def pack(lo, hi, first, keys, values):
    segs = keys.shape[0] // SEG_LEN
    steps = 4
    step = PARTS // steps
    view = (segs // 2, 2, PARTS, GRAN, HD)
    block = (segs // 2, 1, step, GRAN, HD)
    even = pl.BlockSpec(block, lambda i, *s: (0, 0, i, 0, 0))
    odd = pl.BlockSpec(block, lambda i, *s: (0, 1, steps - 1 - i, 0, 0))
    shape = (PARTS, hi - lo, 2 * GRAN, HD)
    keys, values = keys.reshape(view), values.reshape(view)
    return pl.pallas_call(
        functools.partial(pack_kernel, lo, hi),
        grid_spec=pltpu.PrefetchScalarGridSpec(
            num_scalar_prefetch=1,
            grid=(steps,),
            in_specs=[even, odd, even, odd],
            out_specs=pl.BlockSpec((step,) + shape[1:], lambda i, *s: (i, 0, 0, 0)),
        ),
        out_shape=jax.ShapeDtypeStruct(shape, jnp.bfloat16),
        compiler_params=params(60),
        cost_estimate=cost(0, 4 * keys.size * 2),
    )(first, keys, keys, values, values)


def pick_kernel(lo, hi, split, slot_ref, *refs):
    table_ref, out_ref = refs[0], refs[-1]
    devices = out_ref.shape[0]
    slots = slot_ref.shape[1] // PARTS
    base = pl.program_id(0) * devices

    def piece_of(place):
        source, at = place // PARTS, place % PARTS
        piece = table_ref[source, jnp.minimum(at, FIRST - 1)]
        if split:
            rest = refs[1][source, jnp.maximum(at - FIRST, 0)]
            piece = jnp.where(at < FIRST, piece, rest)
        return piece

    def put(d, to, piece):
        out_ref[d, to] = piece

    def guarded(d, carry):
        for n in range(slots):
            slot = (base + d) * slots + n
            to = slot_ref[1, slot]
            pl.when((to >= lo) & (to < hi))(lambda: put(d, to - lo, piece_of(slot_ref[0, slot])))
        return carry

    def plain():
        flat = table_ref.reshape(PARTS * FIRST, 2 * GRAN, HD)
        out = out_ref.reshape(devices * (hi - lo), 2 * GRAN, HD)
        for n0 in range(0, devices * slots, BATCH):
            batch = [base * slots + n for n in range(n0, n0 + BATCH)]
            pieces = [flat[slot_ref[4, slot]] for slot in batch]
            for slot, piece in zip(batch, pieces):
                out[slot_ref[5, slot]] = piece

    most = slot_ref[3, 0]
    if lo == 0 and not split:
        pl.when(most < hi)(plain)
        pl.when(most >= hi)(lambda: lax.fori_loop(0, devices, guarded, None))
    else:
        lax.fori_loop(0, devices, guarded, None)


def pick(lo, hi, slots, tables, after):
    steps = STEPS
    shape = (PARTS, hi - lo, 2 * GRAN, HD)
    return pl.pallas_call(
        functools.partial(pick_kernel, lo, hi, len(tables) > 1),
        grid_spec=pltpu.PrefetchScalarGridSpec(
            num_scalar_prefetch=1,
            grid=(steps,),
            in_specs=[pl.BlockSpec(t.shape, lambda i, *s: (0, 0, 0, 0)) for t in tables]
            + [pl.BlockSpec(memory_space=pl.ANY) for _ in after],
            out_specs=pl.BlockSpec((PARTS // steps,) + shape[1:], lambda i, *s: (i, 0, 0, 0)),
        ),
        out_shape=jax.ShapeDtypeStruct(shape, jnp.bfloat16),
        compiler_params=params(60),
        cost_estimate=cost(0, 4 * tables[0].size),
    )(slots, *tables, *after)


def exchange(x):
    return lax.all_to_all(x, "seq", 0, 0, tiled=True)


def project_kernel(plan, skip, has_acc, is_last, idx_ref, *refs):
    count = sum(len(pieces) for pieces in plan)
    xs = refs[:count]
    wq, wk, wv = refs[count : count + 3]
    rest = refs[count + 3 :]
    start = rest[0] if has_acc else None
    outs = rest[skip + has_acc :]
    acc = outs[-1]
    step = pl.program_id(0)
    nq = wq.shape[1]
    nk = wk.shape[1]
    at = 0
    for s, pieces in enumerate(plan):
        mine = xs[at : at + len(pieces)]
        at += len(pieces)

        @pl.when(step == s)
        def _():
            w_kv = jnp.concatenate([wk[...], wv[...]], axis=1)
            for (lo, hi), x in zip(pieces, mine):
                for w, c, n in ((wq[...], 0, nq), (w_kv, nq, 2 * nk)):
                    d = jnp.dot(x[...], w, preferred_element_type=jnp.float32)
                    if s == 0 and has_acc:
                        acc[lo:hi, c : c + n] = start[lo:hi, c : c + n] + d
                    elif s == 0:
                        acc[lo:hi, c : c + n] = d
                    else:
                        acc[lo:hi, c : c + n] += d
            if is_last and s == len(plan) - 1:
                outs[0][...] = acc[:, :nq].astype(jnp.bfloat16)
                outs[1][...] = acc[:, nq : nq + nk].astype(jnp.bfloat16)
                outs[2][...] = acc[:, nq + nk :].astype(jnp.bfloat16)


def project(idx, first, rows, plan, xs, weights, after, start=None, is_last=False, grant=48):
    depth = xs[0].shape[1]
    nq, nk = weights[0].shape[1], weights[1].shape[1]
    whole = lambda a: pl.BlockSpec(a.shape, lambda i, s: (0, 0))
    weight = lambda n: pl.BlockSpec((depth, n), lambda i, s: (s[first + i], 0))
    result = lambda n: pl.BlockSpec((rows, n), lambda i, s: (0, 0))
    total = nq + 2 * nk
    if is_last:
        out_specs = [result(n) for n in (nq, nk, nk)]
        out_shape = [jax.ShapeDtypeStruct((rows, n), jnp.bfloat16) for n in (nq, nk, nk)]
        scratch = [pltpu.VMEM((rows, total), jnp.float32)]
    else:
        out_specs = result(total)
        out_shape = jax.ShapeDtypeStruct((rows, total), jnp.float32)
        scratch = []
    extra = [] if start is None else [start]
    steps = len(plan)
    return pl.pallas_call(
        functools.partial(project_kernel, plan, len(after), start is not None, is_last),
        grid_spec=pltpu.PrefetchScalarGridSpec(
            num_scalar_prefetch=1,
            grid=(steps,),
            in_specs=[whole(a) for a in xs]
            + [weight(nq), weight(nk), weight(nk)]
            + [whole(a) for a in extra]
            + [pl.BlockSpec(memory_space=pl.ANY) for _ in after],
            out_specs=out_specs,
            scratch_shapes=scratch,
        ),
        out_shape=out_shape,
        compiler_params=params(grant),
        cost_estimate=cost(2 * steps * rows * depth * total, 2 * steps * depth * (total + rows)),
    )(idx, *xs, *weights, *extra, *after)


FAR = DEPTH * SEG_LEN
HEADS = 2


def attend_kernel(slot_ref, q_ref, k_ref, v_ref, *refs):
    *tables, out_ref, keys, values = refs
    scale = math.log2(math.e) / math.sqrt(HD)
    slot = lax.broadcasted_iota(jnp.int32, (1, SEG_LEN), 1)

    def rollout(roll, carry):
        tokens = pl.ds(pl.multiple_of(roll * ROLL, ROLL), ROLL)
        masks = []
        for level in range(DEPTH):
            at = roll * DEPTH + level
            live = slot_ref[PARTS, at]
            row = slot
            if level % 2:
                row = (PARTS - 1 - slot // GRAN) * GRAN + slot % GRAN
            masks.append(jnp.where(row < live, 0.0, -jnp.inf))
            pieces = []
            for i in range(PARTS):
                to = slot_ref[i, at]
                piece = tables[0][i, jnp.minimum(to, SECOND - 1)]
                if len(tables) > 1:
                    rest = tables[1][i, jnp.maximum(to - SECOND, 0)]
                    piece = jnp.where(to < SECOND, piece, rest)
                pieces.append(piece)
            lo = level * SEG_LEN
            keys[lo : lo + SEG_LEN] = jnp.concatenate([p[:GRAN] for p in pieces], axis=0)
            values[lo : lo + SEG_LEN] = jnp.concatenate([p[GRAN:] for p in pieces], axis=0)
        mask = jnp.concatenate(masks, axis=1)
        row = lax.broadcasted_iota(jnp.int32, (ROLL, ROLL), 0)
        causal = jnp.where(row >= lax.broadcasted_iota(jnp.int32, (ROLL, ROLL), 1), 0.0, -jnp.inf)
        causal = jnp.concatenate([causal] * HEADS, axis=0)
        nt = (((1,), (1,)), ((), ()))
        ones = jnp.ones((FAR, HD), jnp.bfloat16)
        for g0 in range(0, GROUP, HEADS):
            heads = range(g0, g0 + HEADS)
            q = jnp.concatenate([q_ref[tokens, g * HD : (g + 1) * HD] for g in heads], axis=0)
            far = lax.dot_general(q, keys[...], nt, preferred_element_type=jnp.float32) + mask
            own = lax.dot_general(q, k_ref[tokens], nt, preferred_element_type=jnp.float32) + causal
            m = jnp.maximum(jnp.max(far, axis=1, keepdims=True), jnp.max(own, axis=1, keepdims=True))
            far = jnp.exp2((far - m) * scale).astype(jnp.bfloat16)
            own = jnp.exp2((own - m) * scale).astype(jnp.bfloat16)
            far_values = jnp.concatenate([values[...], ones], axis=1)
            own_values = jnp.concatenate([v_ref[tokens], ones[:ROLL]], axis=1)
            mix = jnp.dot(far, far_values, preferred_element_type=jnp.float32)
            mix += jnp.dot(own, own_values, preferred_element_type=jnp.float32)
            mix = (mix[:, :HD] / mix[:, HD:]).astype(jnp.bfloat16)
            for n, g in enumerate(heads):
                out_ref[tokens, g * HD : (g + 1) * HD] = mix[n * ROLL : (n + 1) * ROLL]
        return carry

    lax.fori_loop(0, q_ref.shape[0] // ROLL, rollout, None)


def attend(slots, q, k, v, tables):
    vmem = pl.BlockSpec(memory_space=pltpu.VMEM)
    return pl.pallas_call(
        attend_kernel,
        in_specs=[pl.BlockSpec(memory_space=pltpu.SMEM)] + [vmem] * (3 + len(tables)),
        out_specs=vmem,
        scratch_shapes=[
            pltpu.VMEM((FAR, HD), jnp.bfloat16),
            pltpu.VMEM((FAR, HD), jnp.bfloat16),
        ],
        out_shape=jax.ShapeDtypeStruct(q.shape, jnp.bfloat16),
        compiler_params=params(48),
        cost_estimate=cost(
            4 * q.size * (DEPTH * SEG_LEN + ROLL), 4 * (q.size + tables[0].size)
        ),
    )(slots, q, k, v, *tables)


def terms_kernel(count, added, skip, outs, idx_ref, a_ref, b_ref, *refs):
    w_own, w_sib, refs = refs[:count], refs[count : 2 * count], refs[2 * count :]
    more, results = refs[:added], refs[added + skip :]
    for k in range(count):
        acc = jnp.dot(a_ref[...], w_own[k][...], preferred_element_type=jnp.float32)
        acc += jnp.dot(b_ref[...], w_sib[k][...], preferred_element_type=jnp.float32)
        for n, ((which, lo, hi, dtype), out_ref) in enumerate(zip(outs, results)):
            if which == k:
                term = acc[lo:hi]
                if added:
                    term += more[n][...].astype(jnp.float32)
                out_ref[...] = term.astype(dtype)


def terms(idx, first, count, outs, added, after, own, sib, w_own, w_sib):
    rows, depth = own.shape
    width = w_own.shape[1] // (2 * RING)
    cut = 2
    tile = width // cut
    left = pl.BlockSpec((rows, depth), lambda j, s: (0, 0))
    weight = lambda k: pl.BlockSpec((depth, tile), lambda j, s: (0, s[8 + first + k] * cut + j))
    return pl.pallas_call(
        functools.partial(terms_kernel, count, len(added), len(after), outs),
        grid_spec=pltpu.PrefetchScalarGridSpec(
            num_scalar_prefetch=1,
            grid=(cut,),
            in_specs=[left, left]
            + [weight(k) for k in range(count)] * 2
            + [pl.BlockSpec((x.shape[0], tile), lambda j, s: (0, j)) for x in added]
            + [pl.BlockSpec(memory_space=pl.ANY) for _ in after],
            out_specs=[pl.BlockSpec((hi - lo, tile), lambda j, s: (0, j)) for _, lo, hi, _ in outs],
        ),
        out_shape=[jax.ShapeDtypeStruct((hi - lo, width), dtype) for _, lo, hi, dtype in outs],
        compiler_params=params(53),
        cost_estimate=cost(
            4 * count * rows * depth * width, 4 * count * depth * width + 4 * count * rows * width
        ),
    )(idx, own, sib, *([w_own] * count), *([w_sib] * count), *added, *after)


def own_term_kernel(low_rows, own_ref, sib_ref, wa_ref, wb_ref, up_ref, low_ref, top_ref, bottom_ref, w_ref, sems):
    width = w_ref.shape[-1] // 2
    head = lax.axis_index("head")
    loads = []
    for part in range(2):
        at = pl.ds(pl.multiple_of(head * (2 * width) + part * width, width), width)
        to = pl.ds(part * width, width)
        for n, ref in enumerate((wa_ref, wb_ref)):
            loads.append(pltpu.make_async_copy(ref.at[:, at], w_ref.at[n, :, to], sems.at[part, n]))
            loads[-1].start()
    for part in range(2):
        for load in loads[2 * part : 2 * part + 2]:
            load.wait()
        to = slice(part * width, (part + 1) * width)
        acc = jnp.dot(own_ref[...], w_ref[0, :, to], preferred_element_type=jnp.float32)
        acc += jnp.dot(sib_ref[...], w_ref[1, :, to], preferred_element_type=jnp.float32)
        top_ref[:, to] = acc[:low_rows] + up_ref[:, to].astype(jnp.float32)
        bottom_ref[:, to] = acc[low_rows:] + low_ref[:, to].astype(jnp.float32)


def own_term(own, sib, w_own, w_sib, up_top, low_bottom):
    rows, depth = own.shape
    half, width = up_top.shape
    vmem = pl.BlockSpec(memory_space=pltpu.VMEM)
    hbm = pl.BlockSpec(memory_space=pl.ANY)
    return pl.pallas_call(
        functools.partial(own_term_kernel, half),
        in_specs=[vmem, vmem, hbm, hbm, vmem, vmem],
        out_specs=[vmem, vmem],
        out_shape=[jax.ShapeDtypeStruct((half, width), jnp.float32)] * 2,
        scratch_shapes=[
            pltpu.VMEM((2, depth, width), jnp.bfloat16),
            pltpu.SemaphoreType.DMA((2, 2)),
        ],
        compiler_params=params(16),
        cost_estimate=cost(4 * rows * depth * width, 4 * depth * width + 4 * rows * width),
    )(own, sib, w_own, w_sib, up_top, low_bottom)


def add_terms(x, *received):
    for r in received:
        x = x + r.astype(jnp.float32)
    return x.astype(jnp.bfloat16)


def finish_kernel(mine_top, low_top, mine_bottom, up_bottom, out_ref, rows_ref, sems):
    half = mine_top.shape[0]
    tile = half // 2
    stores = []
    for n, (mine, received) in enumerate(((mine_top, low_top), (mine_bottom, up_bottom))):
        for part in range(2):
            rows = slice(part * tile, (part + 1) * tile)
            to = pl.ds(n * half + part * tile, tile)
            total = mine[rows] + received[rows].astype(jnp.float32)
            rows_ref[to] = total.astype(jnp.bfloat16)
            store = pltpu.make_async_copy(rows_ref.at[to], out_ref.at[to], sems.at[n, part])
            store.start()
            stores.append(store)
    for store in stores:
        store.wait()


def finish(mine_top, low_top, mine_bottom, up_bottom):
    vmem = pl.BlockSpec(memory_space=pltpu.VMEM)
    half, width = mine_top.shape
    shape = (2 * half, width)
    return pl.pallas_call(
        finish_kernel,
        in_specs=[vmem] * 4,
        out_specs=pl.BlockSpec(memory_space=pl.ANY),
        out_shape=jax.ShapeDtypeStruct(shape, jnp.bfloat16),
        scratch_shapes=[pltpu.VMEM(shape, jnp.bfloat16), pltpu.SemaphoreType.DMA((2, 2))],
        compiler_params=params(16),
        cost_estimate=cost(0, 16 * mine_top.size),
    )(mine_top, low_top, mine_bottom, up_bottom)


def summed(idx, own, sib, w_own, w_sib):
    rows = own.shape[0]
    half = rows // 2
    f32, b16 = jnp.float32, jnp.bfloat16
    args = (own, sib, w_own, w_sib)
    far_outs = ((0, 0, half, b16), (0, half, rows, b16))
    far_top, far_bottom = terms(idx, 0, 1, far_outs, [], [], *args)
    via_up = send(far_top, UP)
    via_down = send(far_bottom, DOWN)
    near_outs = ((0, 0, half, f32), (0, half, rows, b16), (1, 0, half, b16), (1, half, rows, f32))
    next_top, next_bottom, prev_top, prev_bottom = terms(idx, 1, 2, near_outs, [], [far_top], *args)
    low_bottom = send(next_bottom, UP)
    up_top = send(prev_top, DOWN)
    mine_top, mine_bottom = own_term(*args, up_top, low_bottom)
    low_top = send(add_terms(next_top, via_up), UP)
    up_bottom = send(add_terms(prev_bottom, via_down), DOWN)
    return finish(mine_top, low_top, mine_bottom, up_bottom)


def per_device(
    hidden, w_query, w_key, w_value, w_out, prefix_keys, prefix_values, seg_lengths, ancestors
):
    head = lax.axis_index("head")
    idx = lax.dynamic_index_in_dim(jnp.asarray(index_table()), head, 0, keepdims=False)
    chain = ancestors.reshape(-1)
    rows = hidden.shape[0]
    half = rows // 2
    weights = (w_query, w_key, w_value)
    whole = ((0, rows),)
    split = ((0, half), (half, rows))

    low = send(hidden, UP)
    up = send(hidden, DOWN)
    sib = send(hidden, SIBLING)

    w_sib = send(w_out, SIBLING)

    for_pack, for_pick, for_attend, most = number_pieces(chain, seg_lengths)
    table = exchange(pack(0, FIRST, for_pack, prefix_keys, prefix_values))

    low_half, up_half = low[:half], up[half:]

    def rest():
        return exchange(pack(FIRST, PARTS, for_pack, prefix_keys, prefix_values))

    def pick_all(lo, hi, tables):
        return pick(lo, hi, for_pick, tables, [low_half, up_half, idx])

    picked = lax.cond(
        most[0] > FIRST,
        lambda: pick_all(0, SECOND, [table, rest()]),
        lambda: pick_all(0, SECOND, [table]),
    )
    far = exchange(picked)

    near_blocks = [hidden, sib, low, send(low, SIBLING), up, send(up, SIBLING)]
    acc = project(idx, 0, rows, (whole,) * 6, near_blocks, weights, [])

    far_top, far_bottom = ordered([send(low_half, UP), send(up_half, DOWN)], acc)
    far_blocks = [far_top, far_bottom, send(far_top, SIBLING), send(far_bottom, SIBLING)]
    q, k, v = project(idx, 6, rows, (split,) * 2, far_blocks, weights, [], acc, True, 60)

    def attend_rest():
        far_rest = exchange(pick_all(SECOND, PARTS, [table, rest()]))
        return attend(for_attend, q, k, v, [far, far_rest])

    def attend_all():
        return attend(for_attend, q, k, v, [far])

    own = lax.cond(most[1] > SECOND, attend_rest, attend_all)
    return summed(idx, own, send(own, SIBLING), w_out, w_sib)


def solution(mesh):
    in_specs = (
        P("seq", "head"),
        P(None, "head"),
        P(None, "head"),
        P(None, "head"),
        P("head", None),
        P("seq", "head"),
        P("seq", "head"),
        P(),
        P(),
    )
    out_specs = P("seq", "head")
    return jax.shard_map(
        per_device, mesh=mesh, in_specs=in_specs, out_specs=out_specs, check_vma=False
    )
```
